32 devices in a mesh: dp: 8 (over z, y), tensor: 4 (over x, core).
Axes of the slice: x: 2, y: 2, z: 4, core: 2. Of those that a mesh axis runs over, the one named last changes fastest.
Arguments:
- layer_input: bfloat16 [8192, 768], P(('dp', 'tensor')), may hold values from -6 to 6
- out_grad: bfloat16 [8192, 768], P(('dp', 'tensor')), may hold values from -6 to 6
- attention_norm_scale: float32 [768], replicated, may hold values from 0.5 to 1.5
- expert_norm_scale: float32 [768], replicated, may hold values from 0.5 to 1.5
- query_weight: bfloat16 [768, 768], P('dp', 'tensor'), may hold values from -0.21875 to 0.21875
- key_weight: bfloat16 [768, 768], P('dp', 'tensor'), may hold values from -0.21875 to 0.21875
- value_weight: bfloat16 [768, 768], P('dp', 'tensor'), may hold values from -0.21875 to 0.21875
- output_weight: bfloat16 [768, 768], P('tensor', 'dp'), may hold values from -2.5 to 2.5
- bias_table: float32 [12, 32], replicated, may hold values from -4 to 4
- router_weight: bfloat16 [768, 4], replicated, may hold values from -0.15625 to 0.15625
- expert_in: bfloat16 [4, 768, 3072], P(None, 'dp', 'tensor'), may hold values from -0.21875 to 0.21875
- expert_out: bfloat16 [4, 3072, 768], P(None, 'tensor', 'dp'), may hold values from -0.4375 to 0.4375
- expert_ids: int32 [8192], P('dp'), may hold values from 0 to 3, as said below
- slot_ids: int32 [8192], P('dp'), may hold values from 0 to 511, as said below
- piece_ids: int32 [8192], P('dp'), may hold values from 0 to 2, as said below
- bucket_table: int32 [2047], replicated, may hold values from 0 to 31, as said below
Outputs:
- layer_output: bfloat16 [8192, 768], P(('dp', 'tensor'))
- input_grad: bfloat16 [8192, 768], P(('dp', 'tensor'))
- grad_attn_gain: float32 [768], replicated
- grad_moe_gain: float32 [768], replicated
- grad_query_weight: float32 [768, 768], P('dp', 'tensor')
- grad_key_weight: float32 [768, 768], P('dp', 'tensor')
- grad_value_weight: float32 [768, 768], P('dp', 'tensor')
- grad_output_weight: float32 [768, 768], P('tensor', 'dp')
- grad_bias_table: float32 [12, 32], replicated
- grad_router: float32 [768, 4], replicated
- grad_expert_in: float32 [4, 768, 3072], P(None, 'dp', 'tensor')
- grad_expert_out: float32 [4, 3072, 768], P(None, 'tensor', 'dp')
The draws below stay inside these ranges and needn't reach their ends.
Inputs may be any that keep to these rules, and one draw needn't show every extreme that they name: `expert_ids`: in the 1024 tokens of one sequence no expert is named more than 512 times, and some expert exactly 512 times. `slot_ids`: tokens of one sequence with the same expert have different slots. `piece_ids`: 0 marks text; every sequence holds pieces 1 to 2 in order, each as 256 consecutive tokens. `bucket_table`: entry r + 1023 is the bucket of key position minus query position r; positive r take buckets 32 // 2 and up.
All inputs are finite; a program needn't handle non-finite values.
Results may differ from the reference program's by a relative error of at most 0.023.
Values may be sent and summed in bfloat16 or wider, within the bound.
No kernel may reach another device: no remote copies, remote signals or barrier semaphores. Data moves between devices by JAX's collectives and lax.ppermute only.
A program may use at most 256 MiB of HBM per device.

```python
import jax
import jax.numpy as jnp
from jax import lax

D = 768
HEADS = 12
HEAD_DIM = 64
FF = 3072
BUCKETS = 32
EXPERTS = 4
PIECE = 256
SEQ = 1024
TOKENS = 8192
CAP = 512
NPIECE = 2


def route_draw(key):
    groups = TOKENS // SEQ
    group_keys = jax.random.split(jax.random.fold_in(key, 11), groups)

    def one_group(group_key):
        pick_key, spread_key, order_key = jax.random.split(group_key, 3)
        full_expert = jax.random.randint(pick_key, (), 0, EXPERTS)
        spread = jax.random.permutation(spread_key, (EXPERTS - 1) * CAP)[:SEQ - CAP].astype(jnp.int32)
        other_expert = spread // CAP
        other_expert = other_expert + (other_expert >= full_expert).astype(jnp.int32)
        experts_all = jnp.concatenate([jnp.full((CAP,), full_expert, jnp.int32), other_expert])
        slots_all = jnp.concatenate([jnp.arange(CAP, dtype=jnp.int32), spread % CAP])
        token_order = jax.random.permutation(order_key, SEQ)
        return (experts_all[token_order], slots_all[token_order])
    chosen, slot_rows = jax.vmap(one_group)(group_keys)
    return (chosen.reshape(TOKENS).astype(jnp.int32), slot_rows.reshape(TOKENS).astype(jnp.int32))


def draw_expert_ids(key, part):
    return route_draw(key)[0]


def draw_slot_ids(key, part):
    return route_draw(key)[1]


def draw_piece_ids(key, part):
    groups = TOKENS // SEQ
    group_keys = jax.random.split(jax.random.fold_in(key, 23), groups)

    def one_group(group_key):
        cuts = jnp.sort(jax.random.randint(group_key, (NPIECE,), 0, SEQ - NPIECE * PIECE + 1))
        starts = cuts + jnp.arange(NPIECE, dtype=jnp.int32) * PIECE
        positions = jnp.arange(SEQ, dtype=jnp.int32)
        inside = (positions[:, None] >= starts[None, :]) & (positions[:, None] < starts[None, :] + PIECE)
        numbers = jnp.arange(1, NPIECE + 1, dtype=jnp.int32)
        return jnp.sum(jnp.where(inside, numbers[None, :], 0), axis=1).astype(jnp.int32)
    return jax.vmap(one_group)(group_keys).reshape(TOKENS).astype(jnp.int32)


def draw_bucket_table(key, part):
    half_count = BUCKETS // 2
    exact_count = half_count // 2
    mark_points = jnp.sort(jax.random.permutation(jax.random.fold_in(key, 31), SEQ - exact_count - 1)[:half_count - exact_count - 1].astype(jnp.int32) + exact_count + 1)
    relative = jnp.arange(2 * SEQ - 1, dtype=jnp.int32) - (SEQ - 1)
    magnitude = jnp.abs(relative)
    far_bucket = exact_count + jnp.sum((magnitude[:, None] >= mark_points[None, :]).astype(jnp.int32), axis=1)
    return (jnp.where(magnitude < exact_count, magnitude, far_bucket) + jnp.where(relative > 0, half_count, 0)).astype(jnp.int32)


def spiked(values, own_key, source, target, parts, factor):
    owner, partner = [(jnp.arange(values.shape[axis_at]) // (values.shape[axis_at] // parts)).reshape([-1 if axis == axis_at else 1 for axis in range(values.ndim)]) for axis_at in (source, target)]
    chosen = jax.random.permutation(own_key, parts)[partner]
    strong = (owner == chosen) | (owner == (partner + parts // 2) % parts)
    return jnp.where(strong, factor * values, values)


def steps_of(stream_key, extent, cuts, smallest, high):
    level, own = 1.0, jax.random.fold_in(stream_key, 6)
    for position, shards_of in cuts:
        heights = jnp.exp(jax.random.uniform(jax.random.fold_in(own, position), (shards_of,), jnp.float32, smallest / len(cuts), high / len(cuts)))
        level = level * jnp.repeat(heights, extent[position] // shards_of).reshape([-1 if axis == position else 1 for axis in range(len(extent))])
    return level


def noise(own_key, shape, width, limit, cuts=(), kind=jnp.bfloat16):
    values = jax.random.normal(own_key, shape, jnp.float32) * width
    if len(cuts) > 0:
        values = steps_of(own_key, shape, cuts, -0.22, 0.18) * values
    return jnp.clip(values, min=-limit, max=limit).astype(kind)


def noise_with(key, extent, width, bound, cuts, heavy, kind=jnp.bfloat16):
    entries = width * jax.random.normal(key, extent, jnp.float32)
    if cuts:
        entries = entries * steps_of(key, extent, cuts, -0.22, 0.18)
    return jnp.clip(spiked(entries, jax.random.fold_in(key, 3), *heavy), -bound, bound).astype(kind)


def setup_inputs(seed: int = 0) -> dict:
    keys = jax.random.split(jax.random.key(seed), 17)
    return {
        "layer_input": noise_with(keys[0], (TOKENS, D), 1.0, 6.0, ((0, 32),), (0, 1, 32, 2.75)),
        "out_grad": noise_with(keys[1], (TOKENS, D), 1.0, 6.0, ((0, 32),), (0, 1, 32, 2.75)),
        "attention_norm_scale": jnp.clip(1.0 + 0.1 * jax.random.normal(keys[2], (D,), jnp.float32), 0.5, 1.5),
        "expert_norm_scale": jnp.clip(1.0 + 0.1 * jax.random.normal(keys[3], (D,), jnp.float32), 0.5, 1.5),
        "query_weight": noise(keys[4], (D, HEADS * HEAD_DIM), D ** -0.5, 0.21875, ((0, 8), (1, 4))),
        "key_weight": noise(keys[5], (D, HEADS * HEAD_DIM), D ** -0.5, 0.21875, ((0, 8), (1, 4))),
        "value_weight": noise(keys[6], (D, HEADS * HEAD_DIM), D ** -0.5, 0.21875, ((0, 8), (1, 4))),
        "output_weight": noise(keys[7], (HEADS * HEAD_DIM, D), (max(1, HEADS * HEAD_DIM * 8 // SEQ)) ** -0.5, 2.5, ((0, 4), (1, 8))),
        "bias_table": noise(keys[8], (HEADS, BUCKETS), 1.0, 4.0, (), jnp.float32),
        "router_weight": noise(keys[9], (D, EXPERTS), (2 * D) ** -0.5, 0.15625),
        "expert_in": noise(keys[10], (EXPERTS, D, FF), D ** -0.5, 0.21875, ((1, 8), (2, 4))),
        "expert_out": noise(keys[11], (EXPERTS, FF, D), (FF // 16) ** -0.5, 0.4375, ((1, 4), (2, 8))),
        "expert_ids": draw_expert_ids(jax.random.fold_in(keys[16], 71), 0),
        "slot_ids": draw_slot_ids(jax.random.fold_in(keys[16], 71), 0),
        "piece_ids": draw_piece_ids(jax.random.fold_in(keys[16], 71), 0),
        "bucket_table": draw_bucket_table(jax.random.fold_in(keys[16], 71), 0),
    }


@jax.custom_vjp
def low(v):
    return lax.optimization_barrier(v.astype(jnp.bfloat16)).astype(jnp.float32)

@jax.custom_vjp
def low_back(v):
    return v

def low_keep(v):
    return (low(v), None)

def low_pass(kept, grad):
    return (grad,)

def back_keep(v):
    return (v, None)

def back_low(kept, grad):
    return (low(grad),)
low.defvjp(low_keep, low_pass)
low_back.defvjp(back_keep, back_low)
EPSILON = 1e-06
HIGHEST = lax.Precision.HIGHEST

def rms_norm(matrix_rows, scale_vector_row):
    return matrix_rows * lax.rsqrt(lax.optimization_barrier(jnp.mean(matrix_rows * matrix_rows, axis=-1, keepdims=True)) + EPSILON) * scale_vector_row

def sequence_layer(layer_rows, params, expert_rows, slot_rows, piece_rows, bucket_table):
    attention_norm_scale, expert_norm_scale, query_weight, key_weight, value_weight, output_weight, bias_table, router_weight, expert_in, expert_out = params
    first_normed_rows = low(rms_norm(layer_rows, attention_norm_scale))
    query_rows = low(low_back(jnp.dot(first_normed_rows, query_weight, precision=HIGHEST)))
    key_rows = low(low_back(jnp.dot(first_normed_rows, key_weight, precision=HIGHEST)))
    value_rows = low(low_back(jnp.dot(first_normed_rows, value_weight, precision=HIGHEST)))
    query_heads = query_rows.reshape(SEQ, HEADS, HEAD_DIM)
    key_heads = key_rows.reshape(SEQ, HEADS, HEAD_DIM)
    value_heads = value_rows.reshape(SEQ, HEADS, HEAD_DIM)
    scores = jnp.einsum('qhd,khd->hqk', query_heads, key_heads, precision=HIGHEST) * HEAD_DIM ** (-0.5)
    positions = jnp.arange(SEQ, dtype=jnp.int32)
    rel_index = (positions[None, :] - positions[:, None] + (SEQ - 1)).astype(jnp.int32)
    bucket_rows = jnp.take(bucket_table, rel_index, axis=0)
    scores = low_back(scores + jnp.take(bias_table, bucket_rows, axis=1))
    allowed = (positions[None, :] <= positions[:, None]) | (piece_rows[:, None] == piece_rows[None, :]) & (piece_rows[:, None] > 0)
    scores = jnp.where(allowed[None], scores, -1e+30)
    attn_probs = low(jax.nn.softmax(scores, axis=-1))
    context = jnp.einsum('hqk,khd->qhd', attn_probs, value_heads, precision=HIGHEST).reshape(SEQ, HEADS * HEAD_DIM)
    context = low(low_back(context))
    residual = layer_rows + low_back(jnp.dot(context, output_weight, precision=HIGHEST))
    second_normed_rows = low(rms_norm(low(residual), expert_norm_scale))
    router_probs = jax.nn.softmax(jnp.dot(second_normed_rows, router_weight, precision=HIGHEST), axis=-1)
    gate_value = lax.optimization_barrier(jnp.sum(router_probs * jax.nn.one_hot(expert_rows, EXPERTS, dtype=jnp.float32), axis=-1))
    slot_index = (expert_rows * CAP + slot_rows).astype(jnp.int32)
    dispatched = jnp.zeros((EXPERTS * CAP, D), jnp.float32).at[slot_index].set(second_normed_rows).reshape(EXPERTS, CAP, D)
    pre_act = low_back(jnp.einsum('ecd,edf->ecf', dispatched, expert_in, precision=HIGHEST))
    hidden = low(jax.nn.gelu(pre_act, approximate=True))
    slot_out = low_back(jnp.einsum('ecf,efd->ecd', hidden, expert_out, precision=HIGHEST)).reshape(EXPERTS * CAP, D)
    return residual + gate_value[:, None] * jnp.take(slot_out, slot_index, axis=0)

def reference(layer_input, out_grad, attention_norm_scale, expert_norm_scale, query_weight, key_weight, value_weight, output_weight, bias_table, router_weight, expert_in, expert_out, expert_ids, slot_ids, piece_ids, bucket_table):
    params = tuple((weight.astype(jnp.float32) for weight in (attention_norm_scale, expert_norm_scale, query_weight, key_weight, value_weight, output_weight, bias_table, router_weight, expert_in, expert_out)))
    groups = layer_input.shape[0] // SEQ
    input_groups = layer_input.astype(jnp.float32).reshape(groups, SEQ, D)
    grad_groups = out_grad.astype(jnp.float32).reshape(groups, SEQ, D)
    expert_groups = expert_ids.reshape(groups, SEQ)
    slot_groups = slot_ids.reshape(groups, SEQ)
    piece_groups = piece_ids.reshape(groups, SEQ)

    def group_step(totals, inputs):
        layer_rows, grad_rows, expert_rows, slot_rows, piece_rows = inputs

        def forward(rows_now, weights):
            return sequence_layer(rows_now, weights, expert_rows, slot_rows, piece_rows, bucket_table)
        output_rows, pullback = jax.vjp(forward, layer_rows, params)
        input_rows_grad, weight_grads = pullback(grad_rows)
        totals = jax.tree.map(jnp.add, totals, weight_grads)
        return (totals, (output_rows.astype(jnp.bfloat16), input_rows_grad.astype(jnp.bfloat16)))
    totals, (outputs, input_grads) = lax.scan(group_step, jax.tree.map(jnp.zeros_like, params), (input_groups, grad_groups, expert_groups, slot_groups, piece_groups))
    return (outputs.reshape(TOKENS, D), input_grads.reshape(TOKENS, D), totals[0], totals[1], totals[2], totals[3], totals[4], totals[5], totals[6], totals[7], totals[8], totals[9])
```

```python
import functools

import jax
import jax.numpy as jnp
import numpy as np
from jax import lax
from jax.experimental import pallas as pl
from jax.experimental.pallas import tpu as pltpu
from jax.sharding import PartitionSpec as P

HEAD_DIM = 64
EPSILON = 1e-06
NEG_LARGE = -1e30
HIGHEST = lax.Precision.HIGHEST
BF = jnp.bfloat16
F32 = jnp.float32
NN = (((1,), (0,)), ((), ()))
NT = (((1,), (1,)), ((), ()))
TN = (((0,), (0,)), ((), ()))
VMEM = pl.BlockSpec(memory_space=pltpu.VMEM)
SMEM = pl.BlockSpec(memory_space=pltpu.SMEM)


def mm(left, right, dims, precision=None):
    return lax.dot_general(left, right, dims, preferred_element_type=F32, precision=precision)


def rms_inverse(rows):
    return lax.rsqrt(jnp.mean(rows * rows, axis=-1, keepdims=True) + EPSILON)


def pullback(grad, unit, inverse, gain):
    scaled = grad * gain
    return inverse * (scaled - unit * jnp.mean(scaled * unit, axis=-1, keepdims=True))


def ring_order(size):
    if size == 8:
        return (0, 2, 4, 6, 7, 5, 3, 1)
    return tuple(range(size))


def ring_perms(size):
    order = ring_order(size)
    ahead = [(order[i], order[(i + 1) % size]) for i in range(size)]
    return ahead, [(b, a) for a, b in ahead]


def use_ring(size):
    return size == 8


def ring_gather(chunk, size, far):
    ahead, back = ring_perms(size)
    chunks = [chunk] + [None] * (size - 1)
    up = down = chunk
    for step in range(1, size):
        if step <= far:
            up = lax.ppermute(up, "dp", ahead)
            chunks[size - step] = up
        if step <= size - 1 - far:
            down = lax.ppermute(down, "dp", back)
            chunks[step] = down
    return chunks


def add_low(left, right):
    return (left.astype(F32) + right.astype(F32)).astype(BF)


def ring_scatter(parts, size, far):
    ahead, back = ring_perms(size)
    near = size - 1 - far
    up, down = parts[far], parts[size - near]
    for step in range(max(far, near)):
        if step < far:
            up = lax.ppermute(up, "dp", ahead)
            if step < far - 1:
                up = add_low(up, parts[far - 1 - step])
        if step < near:
            down = lax.ppermute(down, "dp", back)
            if step < near - 1:
                down = add_low(down, parts[size - near + 1 + step])
    return parts[0].astype(F32) + up.astype(F32) + down.astype(F32)


def tensor_perm(flip):
    return [(i, i ^ flip) for i in range(4)]


def swap(value, flip):
    return lax.ppermute(value, "tensor", tensor_perm(flip))


def tensor_gather(rows):
    across = swap(rows, 2)
    beside = swap(rows, 1)
    return rows, beside, across, swap(across, 1)


def tensor_scatter(blocks):
    own_add, across_add = swap(blocks[1], 1), swap(blocks[3], 1)
    across = swap(add_low(blocks[2], across_add), 2)
    return blocks[0], own_add, across


def sum_all(value, size):
    value = value + swap(value, 1)
    value = value + swap(value, 2)
    if size & (size - 1):
        return lax.psum(value, "dp")
    flip = 1
    while flip < size:
        value = value + lax.ppermute(value, "dp", [(i, i ^ flip) for i in range(size)])
        flip *= 2
    return value


def attention_forward_kernel(chunk_count, heads, meta, *refs):
    x_refs, (gain, wheel, piece_row, piece_col) = refs[:4], refs[4:8]
    chunks = refs[8 : 8 + chunk_count]
    part, normed, qkv, ctx, lse, weight, bias = refs[8 + chunk_count :]
    rows = x_refs[0].shape[0]
    blocks = 4
    seq = rows * blocks
    me = meta[0]
    width = heads * HEAD_DIM
    pad = 256
    for k, chunk in enumerate(chunks):
        size = chunk.shape[0]
        at = pl.ds(pl.multiple_of(meta[1 + k] * size, size), size)
        fill = jnp.zeros((size, pad - width), BF)
        whole = chunk[...]
        for s in range(4):
            weight[at, s * pad : (s + 1) * pad] = jnp.concatenate(
                [whole[:, s * width : (s + 1) * width], fill], axis=1
            )
    for k, x_ref in enumerate(x_refs):
        at = pl.ds(pl.multiple_of((me ^ k) * rows, rows), rows)
        wide = x_ref[...].astype(F32)
        low = (wide * rms_inverse(wide) * gain[...]).astype(BF)
        normed[at, :] = low
        out = mm(low, weight[:, : 3 * pad], NN)
        qkv[at, :pad] = (out[:, :pad].astype(BF).astype(F32) * HEAD_DIM**-0.5).astype(BF)
        qkv[at, pad:] = out[:, pad:].astype(BF)
    lane = lax.broadcasted_iota(jnp.int32, (rows, 128), 1)
    ctx[...] = jnp.zeros_like(ctx)
    lse[...] = jnp.zeros_like(lse)

    def head_step(head, carry):
        pair = pl.multiple_of((head // 2) * 128, 128)
        mine = lane // HEAD_DIM == head % 2
        bias[...] = pltpu.roll(
            jnp.broadcast_to(wheel[pl.ds(head, 1), :], (rows, 2 * seq)), 0, 1, stride=1, stride_axis=0
        )
        for b in range(blocks):
            at = slice(b * rows, (b + 1) * rows)
            keys = min(b + 2, blocks) * rows
            q = jnp.where(mine, qkv[at, pl.ds(pair, 128)], jnp.zeros((), BF))
            k = qkv[:keys, pl.ds(pad + pair, 128)]
            v = qkv[:keys, pl.ds(2 * pad + pair, 128)]
            start = (blocks - 1 - b) * rows
            scores = mm(q, k, NT) + bias[:, start : start + keys]
            pieces = []
            if b:
                pieces.append(scores[:, : b * rows])
            tail = scores[:, b * rows :]
            shape = tail.shape
            kept = piece_col[at, :] == piece_row[:, b * rows : keys]
            kept = kept | (
                lax.broadcasted_iota(jnp.int32, shape, 1)
                <= lax.broadcasted_iota(jnp.int32, shape, 0)
            )
            pieces.append(jnp.where(kept, tail, NEG_LARGE))
            scores = jnp.concatenate(pieces, axis=1) if b else pieces[0]
            peak = jnp.max(scores, axis=-1, keepdims=True)
            prob = jnp.exp(scores - peak)
            total = jnp.sum(prob, axis=-1, keepdims=True)
            out = mm(prob.astype(BF), v, NN) / total
            ctx[at, pl.ds(pair, 128)] = jnp.where(mine, out.astype(BF), ctx[at, pl.ds(pair, 128)])
            lse[at, :] = jnp.where(lane == head, peak + jnp.log(total), lse[at, :])
        return carry

    lax.fori_loop(0, heads, head_step, 0)
    for b in range(blocks):
        part[me ^ b] = mm(ctx[b * rows : (b + 1) * rows, :], weight[:, 3 * pad :], NT).astype(BF)


def attention_backward_kernel(owner_count, heads, meta, *refs):
    d_refs, x_refs = refs[:4], refs[4:8]
    gain, reverse, piece_row, piece_col, normed, qkv, ctx, lse, weight = refs[8:17]
    share, gain_grad, diagonals = refs[17:20]
    outs = refs[20 : 20 + owner_count]
    d_resid, d_ctx, lse_row, d_q, d_k, d_v, d_qkv, bias, d_bias, grad = refs[20 + owner_count :]
    rows = d_refs[0].shape[0]
    blocks = 4
    seq = rows * blocks
    me = meta[0]
    width = heads * HEAD_DIM
    pad = 256
    tiles = 2 * blocks - 1
    for k, d_ref in enumerate(d_refs):
        at = pl.ds(pl.multiple_of((me ^ k) * rows, rows), rows)
        low = d_ref[...]
        d_resid[at, :] = low
        d_ctx[at, :] = mm(low, weight[:, 3 * pad :], NN).astype(BF)
    lse_row[...] = jnp.transpose(lse[...])
    lane = lax.broadcasted_iota(jnp.int32, (rows, 128), 1)
    all_lane = lax.broadcasted_iota(jnp.int32, (seq, 128), 1)
    d_q[...] = jnp.zeros_like(d_q)
    d_k[...] = jnp.zeros_like(d_k)
    d_v[...] = jnp.zeros_like(d_v)
    none = jnp.zeros((), BF)

    def head_step(head, carry):
        pair = pl.multiple_of((head // 2) * 128, 128)
        mine = lane // HEAD_DIM == head % 2
        here = pl.ds(pair, 128)
        row = reverse[pl.ds(head, 1), :]
        for a in range(tiles):
            first = 2 * seq - rows * (a + 1)
            ring = jnp.concatenate(
                [row[:, first : first + rows], row[:, first - rows : first]], axis=1
            )
            bias[a] = pltpu.roll(
                jnp.broadcast_to(ring, (rows, 2 * rows)), 0, 1, stride=1, stride_axis=0
            )[:, :rows]
        d_bias[...] = jnp.zeros_like(d_bias)
        for b in range(blocks):
            at = slice(b * rows, (b + 1) * rows)
            q = jnp.where(mine, qkv[at, here], none)
            g = jnp.where(mine, d_ctx[at, here], none)
            base = jnp.sum(
                jnp.transpose(g.astype(F32) * ctx[at, here].astype(F32)), axis=0, keepdims=True
            )
            log_total = lse_row[pl.ds(head, 1), at]
            d_q_block = jnp.zeros((rows, 128), F32)
            for t in range(min(b + 2, blocks)):
                over = slice(t * rows, (t + 1) * rows)
                a = t - b + blocks - 1
                k = qkv[over, pl.ds(pad + pair, 128)]
                scores = mm(k, q, NT) + bias[a]
                prob = jnp.exp(scores - log_total)
                if t >= b:
                    kept = piece_col[over, :] == piece_row[:, at]
                    if t == b:
                        shape = (rows, rows)
                        kept = kept | (
                            lax.broadcasted_iota(jnp.int32, shape, 0)
                            <= lax.broadcasted_iota(jnp.int32, shape, 1)
                        )
                    prob = jnp.where(kept, prob, 0.0)
                d_v[over, here] += mm(prob.astype(BF), g, NN)
                d_prob = mm(qkv[over, pl.ds(2 * pad + pair, 128)], g, NT)
                d_score = (prob * (d_prob - base)).astype(BF)
                d_bias[a] += d_score.astype(F32)
                d_k[over, here] += mm(d_score, q, NN)
                d_q_block += mm(d_score, k, TN)
            d_q[at, here] += jnp.where(mine, d_q_block, 0.0)
        for a in range(tiles):
            total = jnp.zeros((8, 2 * rows), F32)
            for g8 in range(rows // 8):
                piece = jnp.concatenate(
                    [d_bias[a, g8 * 8 : g8 * 8 + 8, :], jnp.zeros((8, rows), F32)], axis=1
                )
                total += pltpu.roll(piece, (2 * rows - g8 * 8) % (2 * rows), 1)
            line = total[0:1]
            for s in range(1, 8):
                line += pltpu.roll(total, 2 * rows - s, 1)[s : s + 1]
            diagonals[pl.ds(head, 1), a * 2 * rows : (a + 1) * 2 * rows] = line
        return carry

    diagonals[...] = jnp.zeros_like(diagonals)
    lax.fori_loop(0, heads, head_step, 0)
    d_qkv[:, :pad] = (d_q[...] * HEAD_DIM**-0.5).astype(BF)
    d_qkv[:, pad : 2 * pad] = d_k[...].astype(BF)
    d_qkv[:, 2 * pad :] = d_v[...].astype(BF)
    total = jnp.zeros(gain_grad.shape, F32)
    for k, x_ref in enumerate(x_refs):
        at = pl.ds(pl.multiple_of((me ^ k) * rows, rows), rows)
        wide = x_ref[...].astype(F32)
        inverse = rms_inverse(wide)
        unit = wide * inverse
        d_normed = mm(d_qkv[at, :], weight[:, : 3 * pad], NT)
        total += jnp.sum(d_normed * unit, axis=0, keepdims=True)
        share[k] = pullback(d_normed, unit, inverse, gain[...]).astype(BF)
    gain_grad[...] = total
    for s in range(3):
        out = mm(normed[...], d_qkv[:, s * pad : (s + 1) * pad], TN)
        grad[:, s * width : (s + 1) * width] = out[:, :width]
    grad[:, 3 * width :] = mm(d_resid[...], ctx[...], TN)[:, :width]
    for k, out in enumerate(outs):
        size = out.shape[0]
        out[...] = grad[pl.ds(pl.multiple_of(meta[1 + k] * size, size), size), :].astype(BF)


def gelu_pair(u):
    c = float(np.sqrt(2.0 / np.pi))
    square = u * u
    t = jnp.tanh(c * u * (1.0 + 0.044715 * square))
    half = 0.5 * (1.0 + t)
    slope = half + 0.5 * c * u * (1.0 - t * t) * (1.0 + 3 * 0.044715 * square)
    return u * half, slope


def route(low, router, expert_col, experts):
    logits = mm(low, router, NN)
    lane = lax.broadcasted_iota(jnp.int32, logits.shape, 1)
    logits = jnp.where(lane < experts, logits, NEG_LARGE)
    grown = jnp.exp(logits - jnp.max(logits, axis=-1, keepdims=True))
    probs = grown / jnp.sum(grown, axis=-1, keepdims=True)
    onehot = (lane == expert_col).astype(F32)
    return probs, onehot, jnp.sum(probs * onehot, axis=-1, keepdims=True)


def moe_kernel(chunk_count, group, experts, capacity, meta, counts, *refs):
    first = group == 0
    last = group == experts // 2 - 1
    r_refs, refs = refs[:4], refs[4:]
    gain, pos_row, pos_col, refs = refs[0], refs[1], refs[2], refs[3:]
    if first:
        g_refs, router, expert_col, refs = refs[:4], refs[4], refs[5], refs[6:]
    else:
        normed, d_token, before_out, before_grad, refs = *refs[:4], refs[4:]
    chunks, refs = refs[:chunk_count], refs[chunk_count:]
    if first:
        normed, d_token, refs = refs[0], refs[1], refs[2:]
    if last:
        out_part, share, gain_grad, refs = refs[0], refs[1], refs[2], refs[3:]
    else:
        out_part, grad_part, refs = refs[0], refs[1], refs[2:]
    outs, refs = refs[:chunk_count], refs[chunk_count:]
    weight, grad, out_slots, grad_slots = refs
    rows, width = r_refs[0].shape
    seq = 4 * rows
    tile = capacity // 2
    for k, chunk in enumerate(chunks):
        size = chunk.shape[1]
        at = pl.ds(pl.multiple_of(meta[1 + k] * size, size), size)
        weight[:, at, :] = chunk[...]
    if first:
        for k in range(4):
            at = slice(k * rows, (k + 1) * rows)
            wide = r_refs[k][...].astype(F32)
            low = (wide * rms_inverse(wide) * gain[...]).astype(BF)
            normed[at, :] = low
            gate = route(low, router[...], expert_col[at, :], experts)[2]
            d_token[at, :] = (gate * g_refs[k][...].astype(F32)).astype(BF)
    slot = lax.broadcasted_iota(jnp.int32, (tile, seq), 0)
    for e in range(2):
        for t in range(2):
            base = ((2 * group + e) * 2 + t) * tile
            at = slice((2 * e + t) * tile, (2 * e + t + 1) * tile)
            used = counts[2 * group + e] > t * tile

            @pl.when(used)
            def _():
                pick = (pos_row[...] == slot + base).astype(F32).astype(BF)
                x = mm(pick, normed[...], NN).astype(BF)
                g = mm(pick, d_token[...], NN).astype(BF)
                hidden, slope = gelu_pair(mm(x, weight[e], NN))
                low = hidden.astype(BF)
                out_slots[at, :] = mm(low, weight[2 + e], NT).astype(BF)
                d_pre = (mm(g, weight[2 + e], NN) * slope).astype(BF)
                grad_slots[at, :] = mm(d_pre, weight[e], NT).astype(BF)
                d_in, d_out = mm(x, d_pre, TN), mm(g, low, TN)
                if t:
                    grad[e] += d_in
                    grad[2 + e] += d_out
                else:
                    grad[e] = d_in
                    grad[2 + e] = d_out

            @pl.when(jnp.logical_not(used))
            def _():
                out_slots[at, :] = jnp.zeros((tile, width), BF)
                grad_slots[at, :] = jnp.zeros((tile, width), BF)
                if not t:
                    grad[e] = jnp.zeros_like(grad[e])
                    grad[2 + e] = jnp.zeros_like(grad[2 + e])

    for k, out in enumerate(outs):
        size = out.shape[1]
        at = pl.ds(pl.multiple_of(meta[1 + k] * size, size), size)
        out[...] = grad[:, at, :].astype(BF)
    if last:
        total = jnp.zeros(gain_grad.shape, F32)
    column = lax.broadcasted_iota(jnp.int32, (rows, 4 * tile), 1) + 4 * group * tile
    for k in range(4):
        at = slice(k * rows, (k + 1) * rows)
        pick = (pos_col[at, :] == column).astype(F32).astype(BF)
        out = mm(pick, out_slots[...], NN)
        d_normed = mm(pick, grad_slots[...], NN)
        if not first:
            out += before_out[k].astype(F32)
            d_normed += before_grad[k].astype(F32)
        out_part[k] = out.astype(BF)
        if last:
            wide = r_refs[k][...].astype(F32)
            inverse = rms_inverse(wide)
            unit = wide * inverse
            total += jnp.sum(d_normed * unit, axis=0, keepdims=True)
            share[k] = pullback(d_normed, unit, inverse, gain[...]).astype(BF)
        else:
            grad_part[k] = d_normed.astype(BF)
    if last:
        gain_grad[...] = total


def join_kernel(
    experts, o0, o1, o2, s0, s1, s2, residual, cotangent, gain, router, expert_col,
    output, d_resid, d_resid_low, small,
):
    expert_own = o0[...].astype(F32) + o1[...].astype(F32) + o2[...].astype(F32)
    wide = residual[...].astype(BF).astype(F32)
    inverse = rms_inverse(wide)
    unit = wide * inverse
    low = (unit * gain[...]).astype(BF)
    probs, onehot, gate = route(low, router[...], expert_col[...], experts)
    output[...] = (residual[...] + gate * expert_own).astype(BF)
    cot = cotangent[...].astype(F32)
    d_gate = jnp.sum(cot * expert_own, axis=-1, keepdims=True)
    d_logits = d_gate * gate * (onehot - probs)
    d_rows = mm(d_logits, router[...].astype(F32), NT, HIGHEST)
    total = cot + s0[...].astype(F32) + s1[...].astype(F32) + s2[...].astype(F32)
    total += pullback(d_rows, unit, inverse, gain[...])
    d_resid[...] = total
    d_resid_low[...] = total.astype(BF)
    small[0:8, :] = mm(d_logits, low.astype(F32), TN, HIGHEST)[:8]
    small[8:9, :] = jnp.sum(d_rows * unit, axis=0, keepdims=True)
    small[9:16, :] = jnp.zeros_like(small[9:16, :])


def call(kernel, outs, operands, scratch, flops, specs=None, limit=60):
    moved = sum(v.size * v.dtype.itemsize for v in operands)
    moved += sum(int(np.prod(s.shape)) * s.dtype.itemsize for s in outs)
    return pl.pallas_call(
        kernel,
        out_shape=outs,
        in_specs=specs,
        out_specs=[VMEM] * len(outs),
        scratch_shapes=scratch,
        compiler_params=pltpu.CompilerParams(vmem_limit_bytes=limit * 2**20),
        cost_estimate=pl.CostEstimate(flops=int(flops), bytes_accessed=moved, transcendentals=0),
    )(*operands)


def shaped(shape, dtype):
    return jax.ShapeDtypeStruct(shape, dtype)


def body(
    layer_input, out_grad, attention_norm_scale, expert_norm_scale, query_weight, key_weight,
    value_weight, output_weight, bias_table, router_weight, expert_in, expert_out, expert_ids,
    slot_ids, piece_ids, bucket_table,
):
    rows, width = layer_input.shape
    me = lax.axis_index("tensor")
    size = lax.axis_size("dp")
    seq = rows * 4
    heads = query_weight.shape[1] // HEAD_DIM
    experts = expert_in.shape[0]
    hidden = expert_in.shape[2]
    capacity = 2 * seq // experts
    buckets = bias_table.shape[1]
    ring = use_ring(size)
    local = heads * HEAD_DIM
    part_rows = query_weight.shape[0]

    qkvo = jnp.concatenate(
        [query_weight, key_weight, value_weight, jnp.transpose(output_weight)], axis=1
    )
    turned = jnp.transpose(expert_out, (0, 2, 1))
    groups = [
        jnp.concatenate([expert_in[2 * g : 2 * g + 2], turned[2 * g : 2 * g + 2]], axis=0)
        for g in range(experts // 2)
    ]
    if ring:
        order = np.array(ring_order(size))
        place = jnp.asarray(np.argsort(order).astype(np.int32))[lax.axis_index("dp")]
        owners = jnp.asarray(order.astype(np.int32))[(place + jnp.arange(size)) % size]
        qkvo_chunks = ring_gather(qkvo, size, size // 2)
        group_chunks = [
            ring_gather(c, size, size // 2 - 1 + g % 2) for g, c in enumerate(groups)
        ]
    else:
        owners = jnp.zeros((1,), jnp.int32)
        qkvo_chunks = [lax.all_gather(qkvo, "dp", axis=0, tiled=True)]
        group_chunks = [[lax.all_gather(c, "dp", axis=1, tiled=True)] for c in groups]
    count = len(owners)
    span = width // count
    meta = jnp.concatenate([me[None].astype(jnp.int32), owners.astype(jnp.int32)])

    x_pieces = tensor_gather(layer_input)
    g_pieces = tensor_gather(out_grad)
    flips = me ^ jnp.arange(4)
    expert_seen = expert_ids.reshape(4, rows)[flips].reshape(seq)
    chosen = (expert_seen[:, None] == jnp.arange(experts)[None, :]).astype(BF)
    earlier = jnp.tril(jnp.ones((seq, seq), BF), -1)
    rank = jnp.sum(jnp.dot(earlier, chosen, preferred_element_type=F32) * chosen, axis=1)
    pos = expert_seen * capacity + rank.astype(jnp.int32)
    counts = jnp.sum(chosen.astype(F32), axis=0).astype(jnp.int32)
    pos_row, pos_col = pos[None, :], pos[:, None]
    expert_col = expert_seen[:, None]
    piece_row = jnp.where(piece_ids > 0, piece_ids, -1)[None, :]
    piece_col = jnp.where(piece_ids > 0, piece_ids, -2)[:, None]

    none = jnp.full((1,), -1, jnp.int32)
    backward_order = jnp.concatenate([none, bucket_table[::-1]])
    listed = jnp.concatenate(
        [bucket_table[rows - 1 :], none, bucket_table[: rows - 1], backward_order]
    )
    spread = (jnp.arange(buckets)[:, None] == listed[None, :]).astype(F32)
    bias_local = lax.dynamic_slice_in_dim(bias_table, me * heads, heads, 0)
    rel = jnp.dot(jnp.pad(bias_local, ((0, 8 - heads), (0, 0))), spread, precision=HIGHEST)
    wheel, reverse = rel[:, : 2 * seq], rel[:, 2 * seq :]

    attn_gain = attention_norm_scale[None, :]
    moe_gain = expert_norm_scale[None, :]
    router = jnp.pad(router_weight, ((0, 0), (0, 128 - experts)))

    part, normed_one, qkv, ctx, lse, weight = call(
        functools.partial(attention_forward_kernel, count, heads),
        [
            shaped((4, rows, width), BF), shaped((seq, width), BF), shaped((seq, 768), BF),
            shaped((seq, 256), BF), shaped((seq, 128), F32), shaped((width, 1024), BF),
        ],
        [meta, *x_pieces, attn_gain, wheel, piece_row, piece_col, *qkvo_chunks],
        [pltpu.VMEM((rows, 2 * seq), F32)],
        12e9,
        [SMEM] + [VMEM] * (8 + count),
    )
    a0, a1, a2 = tensor_scatter(part)
    residual = (
        layer_input.astype(F32) + (a0.astype(F32) + a1.astype(F32) + a2.astype(F32))
    )
    r_pieces = tensor_gather(residual.astype(BF))

    group_grads = []
    for g in range(experts // 2):
        first, last = g == 0, g == experts // 2 - 1
        operands = [meta, counts, *r_pieces, moe_gain, pos_row, pos_col]
        outs = []
        if first:
            operands += [*g_pieces, router, expert_col]
            outs += [shaped((seq, width), BF)] * 2
        else:
            operands += [normed_two, d_token, out_part, grad_part]
        operands += group_chunks[g]
        outs += [shaped((4, rows, width), BF)] * 2
        if last:
            outs += [shaped((1, width), F32)]
        outs += [shaped((4, span, hidden), BF)] * count
        results = call(
            functools.partial(moe_kernel, count, g, experts, capacity),
            outs,
            operands,
            [
                pltpu.VMEM((4, width, hidden), BF),
                pltpu.VMEM((4, width, hidden), F32),
                pltpu.VMEM((2 * capacity, width), BF),
                pltpu.VMEM((2 * capacity, width), BF),
            ],
            12e9,
            [SMEM] * 2 + [VMEM] * (len(operands) - 2),
        )
        if first:
            normed_two, d_token, results = results[0], results[1], results[2:]
        if last:
            out_part, share, moe_gain_grad, results = *results[:3], results[3:]
        else:
            out_part, grad_part, results = results[0], results[1], results[2:]
        group_grads.append(results)

    o0, o1, o2 = tensor_scatter(out_part)
    s0, s1, s2 = tensor_scatter(share)
    layer_output, d_resid, d_resid_low, small = call(
        functools.partial(join_kernel, experts),
        [
            shaped((rows, width), BF), shaped((rows, width), F32), shaped((rows, width), BF),
            shaped((16, width), F32),
        ],
        [o0, o1, o2, s0, s1, s2, residual, out_grad, moe_gain, router, expert_col[:rows]],
        [],
        1e9,
        [VMEM] * 11,
    )
    d_pieces = tensor_gather(d_resid_low)

    tiles = 7
    results = call(
        functools.partial(attention_backward_kernel, count, heads),
        [
            shaped((4, rows, width), BF), shaped((1, width), F32),
            shaped((8, tiles * 2 * rows), F32),
            *[shaped((span, 4 * local), BF)] * count,
        ],
        [
            meta, *d_pieces, *x_pieces, attn_gain, reverse, piece_row, piece_col, normed_one, qkv,
            ctx, lse, weight,
        ],
        [
            pltpu.VMEM((seq, width), BF),
            pltpu.VMEM((seq, 256), BF),
            pltpu.VMEM((128, seq), F32),
            pltpu.VMEM((seq, 256), F32),
            pltpu.VMEM((seq, 256), F32),
            pltpu.VMEM((seq, 256), F32),
            pltpu.VMEM((seq, 768), BF),
            pltpu.VMEM((tiles, rows, rows), F32),
            pltpu.VMEM((tiles, rows, rows), F32),
            pltpu.VMEM((width, 4 * local), F32),
        ],
        20e9,
        [SMEM] + [VMEM] * 17,
    )
    share, attn_gain_grad, diagonals = results[:3]
    qkvo_grads = results[3:]
    i0, i1, i2 = tensor_scatter(share)
    input_grad = (
        d_resid + (i0.astype(F32) + i1.astype(F32) + i2.astype(F32))
    ).astype(BF)

    total = 2 * seq
    tile_buckets = []
    for a in range(tiles):
        start = total - rows * (a + 1)
        tile_buckets += [
            backward_order[start : start + rows], backward_order[start - rows : start]
        ]
    collect = (
        jnp.concatenate(tile_buckets)[:, None] == jnp.arange(buckets)[None, :]
    ).astype(F32)
    grad_bias = jnp.dot(diagonals[:heads], collect, precision=HIGHEST)
    head_count = bias_table.shape[0]
    grad_bias = lax.dynamic_update_slice_in_dim(
        jnp.zeros_like(bias_table), grad_bias, me * heads, 0
    )
    flat = jnp.pad(grad_bias.reshape(1, -1), ((0, 0), (0, width - head_count * buckets)))
    sums = sum_all(
        jnp.concatenate(
            [
                small[:experts], moe_gain_grad + small[8:9], attn_gain_grad, flat,
                jnp.zeros((1, width), F32),
            ],
            axis=0,
        ),
        size,
    )
    grad_router = jnp.transpose(sums[:experts])
    grad_moe_gain = sums[experts]
    grad_attn_gain = sums[experts + 1]
    grad_bias_table = sums[experts + 2, : head_count * buckets].reshape(head_count, buckets)

    def owned(parts, far, axis):
        if ring:
            return ring_scatter(parts, size, far)
        return lax.psum_scatter(parts[0].astype(F32), "dp", scatter_dimension=axis, tiled=True)

    expert_grads = [
        owned(parts, size // 2 - 1 + g % 2, 1) for g, parts in enumerate(group_grads)
    ]
    qkvo_grad = owned(qkvo_grads, size // 2, 0)
    grad_query, grad_key, grad_value = (
        qkvo_grad[:, s * local : (s + 1) * local] for s in range(3)
    )
    grad_output = jnp.transpose(qkvo_grad[:, 3 * local :])
    grad_in = jnp.concatenate([v[:2] for v in expert_grads], axis=0)
    grad_out = jnp.transpose(jnp.concatenate([v[2:] for v in expert_grads], axis=0), (0, 2, 1))
    return (
        layer_output, input_grad, grad_attn_gain, grad_moe_gain, grad_query, grad_key, grad_value,
        grad_output, grad_bias_table, grad_router, grad_in, grad_out,
    )


def solution(mesh):
    in_specs = (
        P(("dp", "tensor"), None),
        P(("dp", "tensor"), None),
        P(),
        P(),
        P("dp", "tensor"),
        P("dp", "tensor"),
        P("dp", "tensor"),
        P("tensor", "dp"),
        P(),
        P(),
        P(None, "dp", "tensor"),
        P(None, "tensor", "dp"),
        P("dp"),
        P("dp"),
        P("dp"),
        P(),
    )
    out_specs = (
        P(("dp", "tensor"), None),
        P(("dp", "tensor"), None),
        P(),
        P(),
        P("dp", "tensor"),
        P("dp", "tensor"),
        P("dp", "tensor"),
        P("tensor", "dp"),
        P(),
        P(),
        P(None, "dp", "tensor"),
        P(None, "tensor", "dp"),
    )
    return jax.shard_map(body, mesh=mesh, in_specs=in_specs, out_specs=out_specs, check_vma=False)
```

```python
import functools

import jax
import jax.numpy as jnp
import numpy as np
from jax import lax
from jax.experimental import pallas as pl
from jax.experimental.pallas import tpu as pltpu
from jax.sharding import PartitionSpec as P

HEAD_DIM = 64
EPSILON = 1e-06
NEG_LARGE = -1e30
HIGHEST = lax.Precision.HIGHEST
BF = jnp.bfloat16
F32 = jnp.float32
NN = (((1,), (0,)), ((), ()))
NT = (((1,), (1,)), ((), ()))
TN = (((0,), (0,)), ((), ()))
VMEM = pl.BlockSpec(memory_space=pltpu.VMEM)
GROUPS = ((0, 1), (2, 3))
VMEM_MIB = {
    "pack": 8, "prepare": 12, "attention_forward": 28, "moe": 30, "moe_last": 30, "join": 14,
    "attention_backward0": 24, "attention_backward1": 28, "input_share": 16, "finish": 16,
}


def mm(left, right, dims, precision=None):
    return lax.dot_general(left, right, dims, preferred_element_type=F32, precision=precision)


def rms_inverse(rows):
    return lax.rsqrt(jnp.mean(rows * rows, axis=-1, keepdims=True) + EPSILON)


def pullback(grad, unit, inverse, gain):
    scaled = grad * gain
    return inverse * (scaled - unit * jnp.mean(scaled * unit, axis=-1, keepdims=True))


def tie(value, *others):
    if not others:
        return value
    return lax.optimization_barrier((value, *others))[0]


def ring_order(size):
    if size == 8:
        return (0, 2, 4, 6, 7, 5, 3, 1)
    return tuple(range(size))


def ring_perms(size):
    order = ring_order(size)
    ahead = [(order[i], order[(i + 1) % size]) for i in range(size)]
    return ahead, [(b, a) for a, b in ahead]


def use_ring(size):
    return size == 8


def ring_gather(chunk, size, far, name):
    ahead, back = ring_perms(size)
    chunks = [chunk] + [None] * (size - 1)
    up = down = chunk
    for step in range(1, size):
        if step <= far:
            with jax.named_scope(f"{name}_up{step}"):
                up = lax.ppermute(up, "dp", ahead)
            chunks[size - step] = up
        if step <= size - 1 - far:
            with jax.named_scope(f"{name}_down{step}"):
                down = lax.ppermute(down, "dp", back)
            chunks[step] = down
    return chunks


def add_low(left, right):
    return (left.astype(F32) + right.astype(F32)).astype(BF)


def ring_scatter(parts, size, far, name):
    ahead, back = ring_perms(size)
    near = size - 1 - far
    up, down = parts[far], parts[size - near]
    for step in range(max(far, near) + 1):
        wait = yield up, down
        if step < far:
            if step:
                up = add_low(up, parts[far - step])
            with jax.named_scope(f"{name}_up{step + 1}"):
                up = lax.ppermute(tie(up, *wait), "dp", ahead)
        if step < near:
            if step:
                down = add_low(down, parts[size - near + step])
            with jax.named_scope(f"{name}_down{step + 1}"):
                down = lax.ppermute(tie(down, *wait), "dp", back)


def tensor_perm(flip):
    return [(i, i ^ flip) for i in range(4)]


def swap(value, flip):
    return lax.ppermute(value, "tensor", tensor_perm(flip))


def tensor_gather(rows, name):
    with jax.named_scope(name):
        across = swap(rows, 2)
        beside = swap(rows, 1)
        return rows, beside, across, swap(across, 1)


def tensor_scatter(keep, send, name):
    with jax.named_scope(name):
        got = swap(send, 1)
        return keep, got, swap(add_low(keep[1], got[1]), 2)


def owner_at(k, count):
    if count == 1:
        return 0
    me = lax.axis_index("dp")
    place = lax.rem(jnp.where(lax.rem(me, 2) == 0, me // 2, 7 - me // 2) + k, 8)
    return jnp.where(place < 4, 2 * place, 15 - 2 * place)


def owned_rows(k, count, size):
    return pl.ds(pl.multiple_of(owner_at(k, count) * size, size), size)


def pack_kernel(groups, query, key, value, output, w_in, w_out, out, *packed):
    out[...] = jnp.concatenate(
        [query[...], key[...], value[...], jnp.transpose(output[...].astype(F32)).astype(BF)], axis=1
    )
    for chosen, part in zip(groups, packed):
        for i, e in enumerate(chosen):
            part[i] = w_in[e]
            part[len(chosen) + i] = w_out[e]


def finish_kernel(groups, *refs):
    terms, (d_in, d_out) = refs[:-2], refs[-2:]
    for g, chosen in enumerate(groups):
        own, up, down = terms[3 * g : 3 * g + 3]
        for i in range(2 * len(chosen)):
            total = own[i].astype(F32) + up[i].astype(F32) + down[i].astype(F32)
            if i < len(chosen):
                d_in[chosen[i]] = total
            else:
                d_out[chosen[i - len(chosen)]] = total


def prepare_kernel(heads, experts, capacity, ids, pieces, buckets, table, rows, cols, wheel):
    seq = ids.shape[1]
    part = seq // 4
    me = lax.axis_index("tensor")
    seen = jnp.concatenate(
        [ids[:, pl.ds(pl.multiple_of((me ^ k) * part, part), part)] for k in range(4)], axis=1
    )
    chosen = lax.broadcasted_iota(jnp.int32, (8, seq), 0) == seen
    chosen = chosen.astype(F32)
    shape = (seq, seq)
    earlier = lax.broadcasted_iota(jnp.int32, shape, 0) < lax.broadcasted_iota(jnp.int32, shape, 1)
    rank = mm(chosen.astype(BF), earlier.astype(F32).astype(BF), NN)
    pos = jnp.sum(rank * chosen, axis=0, keepdims=True) + (seen * capacity).astype(F32)
    piece = pieces[...].astype(F32)
    held = jnp.concatenate(
        [pos, seen.astype(F32), jnp.where(piece > 0, piece, -1.0), jnp.zeros((5, seq), F32)], axis=0
    )
    rows[...] = held
    cols[...] = jnp.transpose(held)
    bucket = pltpu.roll(buckets[...], 2 * seq - (part - 1), 1)
    spread = lax.broadcasted_iota(jnp.int32, (table.shape[1], 2 * seq), 0) == bucket
    local = [table[pl.ds(me * heads + h, 1), :] for h in range(heads)]
    local.append(jnp.zeros((8 - heads, table.shape[1]), F32))
    wheel[...] = mm(jnp.concatenate(local, axis=0), spread.astype(F32), NN, HIGHEST)


def sum_all(value, size):
    value = value + swap(value, 1)
    value = value + swap(value, 2)
    if size & (size - 1):
        return lax.psum(value, "dp")
    flip = 1
    while flip < size:
        value = value + lax.ppermute(value, "dp", [(i, i ^ flip) for i in range(size)])
        flip *= 2
    return value


def attention_forward_kernel(chunk_count, heads, *refs):
    x_refs, (gain, wheel, info_rows, info_cols) = refs[:4], refs[4:8]
    chunks = refs[8 : 8 + chunk_count]
    keep, send, normed, qkv, ctx, lse, weight, bias, part = refs[8 + chunk_count :]
    rows = x_refs[0].shape[0]
    blocks = 4
    seq = rows * blocks
    me = lax.axis_index("tensor")
    width = heads * HEAD_DIM
    pad = 256
    for k, chunk in enumerate(chunks):
        size = chunk.shape[0]
        at = owned_rows(k, chunk_count, size)
        fill = jnp.zeros((size, pad - width), BF)
        whole = chunk[...]
        for s in range(4):
            weight[at, s * pad : (s + 1) * pad] = jnp.concatenate(
                [whole[:, s * width : (s + 1) * width], fill], axis=1
            )
    for k, x_ref in enumerate(x_refs):
        at = pl.ds(pl.multiple_of((me ^ k) * rows, rows), rows)
        wide = x_ref[...].astype(F32)
        low = (wide * rms_inverse(wide) * gain[...]).astype(BF)
        normed[at, :] = low
        out = mm(low, weight[:, : 3 * pad], NN)
        qkv[at, :pad] = (out[:, :pad].astype(BF).astype(F32) * HEAD_DIM**-0.5).astype(BF)
        qkv[at, pad:] = out[:, pad:].astype(BF)
    lane = lax.broadcasted_iota(jnp.int32, (rows, 128), 1)
    ctx[...] = jnp.zeros_like(ctx)
    lse[...] = jnp.zeros_like(lse)

    def head_step(head, carry):
        pair = pl.multiple_of((head // 2) * 128, 128)
        mine = lane // HEAD_DIM == head % 2
        bias[...] = pltpu.roll(
            jnp.broadcast_to(wheel[pl.ds(head, 1), :], (rows, 2 * seq)), 0, 1, stride=1, stride_axis=0
        )
        for b in range(blocks):
            at = slice(b * rows, (b + 1) * rows)
            keys = min(b + 2, blocks) * rows
            q = jnp.where(mine, qkv[at, pl.ds(pair, 128)], jnp.zeros((), BF))
            k = qkv[:keys, pl.ds(pad + pair, 128)]
            v = qkv[:keys, pl.ds(2 * pad + pair, 128)]
            start = (blocks - 1 - b) * rows
            scores = mm(q, k, NT) + bias[:, start : start + keys]
            pieces = []
            if b:
                pieces.append(scores[:, : b * rows])
            tail = scores[:, b * rows :]
            shape = tail.shape
            piece = info_cols[at, 2:3]
            kept = (piece == info_rows[2:3, b * rows : keys]) & (piece > 0)
            kept = kept | (
                lax.broadcasted_iota(jnp.int32, shape, 1)
                <= lax.broadcasted_iota(jnp.int32, shape, 0)
            )
            pieces.append(jnp.where(kept, tail, NEG_LARGE))
            scores = jnp.concatenate(pieces, axis=1) if b else pieces[0]
            peak = jnp.max(scores, axis=-1, keepdims=True)
            prob = jnp.exp(scores - peak)
            total = jnp.sum(prob, axis=-1, keepdims=True)
            out = mm(prob.astype(BF), v, NN) / total
            ctx[at, pl.ds(pair, 128)] = jnp.where(mine, out.astype(BF), ctx[at, pl.ds(pair, 128)])
            lse[at, :] = jnp.where(lane == head, peak + jnp.log(total), lse[at, :])
        return carry

    lax.fori_loop(0, heads, head_step, 0)
    for b in range(blocks):
        part[me ^ b] = mm(ctx[b * rows : (b + 1) * rows, :], weight[:, 3 * pad :], NT).astype(BF)
    for k in range(2):
        keep[k] = part[2 * k]
        send[k] = part[2 * k + 1]


def attention_backward_kernel(owner_count, heads, pair_index, *refs):
    last = pair_index == 1
    d_refs, (wheel, buckets, info_rows, info_cols, qkv, ctx, lse, weight) = refs[:4], refs[4:12]
    refs = refs[12:]
    if last:
        normed, before, bias_before, d_qkv, bias_grad, refs = *refs[:5], refs[5:]
        outs, refs = refs[:owner_count], refs[owner_count:]
        grad, d_resid, refs = refs[0], refs[1], refs[2:]
    else:
        d_part, bias_grad, refs = refs[0], refs[1], refs[2:]
    d_ctx, lse_row, d_q, d_k, d_v, slope, bias, d_bias = refs
    rows = d_refs[0].shape[0]
    blocks = 4
    seq = rows * blocks
    me = lax.axis_index("tensor")
    width = heads * HEAD_DIM
    pad = 256
    tiles = 2 * blocks - 1
    pair = 128 * pair_index
    here = slice(pair, pair + 128)
    for k, d_ref in enumerate(d_refs):
        at = pl.ds(pl.multiple_of((me ^ k) * rows, rows), rows)
        low = d_ref[...]
        if last:
            d_resid[at, :] = low
        d_ctx[at, :] = mm(low, weight[:, 3 * pad + pair : 3 * pad + pair + 128], NN).astype(BF)
    lse_row[...] = jnp.transpose(lse[...])
    lane = lax.broadcasted_iota(jnp.int32, (rows, 128), 1)
    d_q[...] = jnp.zeros_like(d_q)
    d_k[...] = jnp.zeros_like(d_k)
    d_v[...] = jnp.zeros_like(d_v)
    bias_grad[...] = bias_before[...] if last else jnp.zeros_like(bias_grad)
    none = jnp.zeros((), BF)
    bucket = pltpu.roll(buckets[...], 2 * seq - (rows - 1), 1)
    spread = lax.broadcasted_iota(jnp.int32, (bias_grad.shape[0], 2 * seq), 0) == bucket
    head_lane = lax.broadcasted_iota(jnp.int32, bias_grad.shape, 1)

    def head_step(head, carry):
        mine = lane // HEAD_DIM == head % 2
        slope[...] = pltpu.roll(
            jnp.broadcast_to(wheel[pl.ds(head, 1), :], (rows, 2 * seq)), 0, 1, stride=1, stride_axis=0
        )
        for a in range(tiles):
            bias[a] = jnp.transpose(slope[:, a * rows : (a + 1) * rows])
        d_bias[...] = jnp.zeros_like(d_bias)
        for b in range(blocks):
            at = slice(b * rows, (b + 1) * rows)
            q = jnp.where(mine, qkv[at, here], none)
            g = jnp.where(mine, d_ctx[at, :], none)
            base = jnp.sum(
                jnp.transpose(g.astype(F32) * ctx[at, here].astype(F32)), axis=0, keepdims=True
            )
            log_total = lse_row[pl.ds(head, 1), at]
            d_q_block = jnp.zeros((rows, 128), F32)
            for t in range(min(b + 2, blocks)):
                over = slice(t * rows, (t + 1) * rows)
                a = t - b + blocks - 1
                k = qkv[over, pad + pair : pad + pair + 128]
                scores = mm(k, q, NT) + bias[a]
                prob = jnp.exp(scores - log_total)
                if t >= b:
                    piece = info_cols[over, 2:3]
                    kept = (piece == info_rows[2:3, at]) & (piece > 0)
                    if t == b:
                        shape = (rows, rows)
                        kept = kept | (
                            lax.broadcasted_iota(jnp.int32, shape, 0)
                            <= lax.broadcasted_iota(jnp.int32, shape, 1)
                        )
                    prob = jnp.where(kept, prob, 0.0)
                d_v[over, :] += mm(prob.astype(BF), g, NN)
                d_prob = mm(qkv[over, 2 * pad + pair : 2 * pad + pair + 128], g, NT)
                d_score = (prob * (d_prob - base)).astype(BF)
                d_bias[a] += d_score.astype(F32)
                d_k[over, :] += mm(d_score, q, NN)
                d_q_block += mm(d_score, k, TN)
            d_q[at, :] += jnp.where(mine, d_q_block, 0.0)
        for a in range(tiles):
            slope[:, a * rows : (a + 1) * rows] = jnp.transpose(d_bias[a])
        slope[:, tiles * rows :] = jnp.zeros((rows, rows), F32)
        total = jnp.zeros((8, 2 * seq), F32)
        for g8 in range(rows // 8):
            total += pltpu.roll(slope[g8 * 8 : g8 * 8 + 8, :], (2 * seq - g8 * 8) % (2 * seq), 1)
        line = total[0:1]
        for s in range(1, 8):
            line += pltpu.roll(total, 2 * seq - s, 1)[s : s + 1]
        column = jnp.sum(jnp.where(spread, line, 0.0), axis=1, keepdims=True)
        bias_grad[...] = jnp.where(head_lane == me * heads + head, column, bias_grad[...])
        return carry

    lax.fori_loop(2 * pair_index, min(heads, 2 * pair_index + 2), head_step, 0)
    for s, value in enumerate((d_q[...] * HEAD_DIM**-0.5, d_k[...], d_v[...])):
        if last:
            d_qkv[:, s * pad : s * pad + pair] = before[:, s * 128 : (s + 1) * 128]
            d_qkv[:, s * pad + pair : (s + 1) * pad] = value.astype(BF)
        else:
            d_part[:, s * 128 : (s + 1) * 128] = value.astype(BF)
    if not last:
        return
    for s in range(3):
        out = mm(normed[...], d_qkv[:, s * pad : (s + 1) * pad], TN)
        grad[:, s * width : (s + 1) * width] = out[:, :width]
    grad[:, 3 * width :] = mm(d_resid[...], ctx[...], TN)[:, :width]
    for k, out in enumerate(outs):
        out[...] = grad[owned_rows(k, owner_count, out.shape[0]), :].astype(BF)


def input_share_kernel(experts, *refs):
    x_refs = refs[:4]
    gain, d_qkv, weight, small, moe_gain_grad, bias_grad, keep, send, sums = refs[4:]
    rows, width = x_refs[0].shape
    me = lax.axis_index("tensor")
    total = jnp.zeros((1, width), F32)
    for k, x_ref in enumerate(x_refs):
        at = pl.ds(pl.multiple_of((me ^ k) * rows, rows), rows)
        wide = x_ref[...].astype(F32)
        inverse = rms_inverse(wide)
        unit = wide * inverse
        d_normed = mm(d_qkv[at, :], weight[:, :768], NT)
        total += jnp.sum(d_normed * unit, axis=0, keepdims=True)
        share = pullback(d_normed, unit, inverse, gain[...]).astype(BF)
        (send if k % 2 else keep)[k // 2] = share
    lines = [total, moe_gain_grad[...] + small[8:9, :]] + [small[e : e + 1, :] for e in range(experts)]
    per = width // 128
    for i, line in enumerate(lines):
        for j in range(per):
            sums[i * per + j : i * per + j + 1, :] = line[:, j * 128 : (j + 1) * 128]
    first = len(lines) * per
    count = bias_grad.shape[0]
    sums[first : first + count, :] = bias_grad[...]
    sums[first + count :, :] = jnp.zeros_like(sums[first + count :, :])


def gelu_pair(u):
    c = float(np.sqrt(2.0 / np.pi))
    square = u * u
    t = jnp.tanh(c * u * (1.0 + 0.044715 * square))
    half = 0.5 * (1.0 + t)
    slope = half + 0.5 * c * u * (1.0 - t * t) * (1.0 + 3 * 0.044715 * square)
    return u * half, slope


def route(low, router, expert_col, experts):
    logits = mm(low, router, NN)
    lane = lax.broadcasted_iota(jnp.int32, logits.shape, 1)
    logits = jnp.where(lane < experts, logits, NEG_LARGE)
    grown = jnp.exp(logits - jnp.max(logits, axis=-1, keepdims=True))
    probs = grown / jnp.sum(grown, axis=-1, keepdims=True)
    onehot = (lane == expert_col).astype(F32)
    return probs, onehot, jnp.sum(probs * onehot, axis=-1, keepdims=True)


def moe_kernel(chunk_count, chosen, first, last, experts, capacity, *refs):
    kinds = len(chosen)
    r_refs, refs = refs[:4], refs[4:]
    gain, info_rows, info_cols, refs = refs[0], refs[1], refs[2], refs[3:]
    if first:
        g_refs, router, refs = refs[:4], refs[4], refs[5:]
    else:
        normed, d_token, before, refs = refs[0], refs[1], refs[2:4], refs[4:]
    chunks, refs = refs[:chunk_count], refs[chunk_count:]
    if first:
        normed, d_token, refs = refs[0], refs[1], refs[2:]
    if last:
        out_keep, out_send, keep, send, gain_grad, refs = *refs[:5], refs[5:]
    else:
        out_part, grad_part, refs = refs[0], refs[1], refs[2:]
    outs, refs = refs[:chunk_count], refs[chunk_count:]
    weight, grad, out_slots, grad_slots = refs
    rows, width = r_refs[0].shape
    seq = 4 * rows
    tile = capacity // 2
    if first:
        for k in range(4):
            at = slice(k * rows, (k + 1) * rows)
            wide = r_refs[k][...].astype(F32)
            low = (wide * rms_inverse(wide) * gain[...]).astype(BF)
            normed[at, :] = low
            gate = route(low, router[...], info_cols[at, 1:2], experts)[2]
            d_token[at, :] = (gate * g_refs[k][...].astype(F32)).astype(BF)
    slot = lax.broadcasted_iota(jnp.int32, (tile, seq), 0).astype(F32)
    for i, e in enumerate(chosen):
        held = jnp.sum((info_rows[1:2, :] == e).astype(F32))
        for k, chunk in enumerate(chunks):
            place = owned_rows(k, chunk_count, chunk.shape[1])
            weight[0, place, :] = chunk[i]
            weight[1, place, :] = chunk[kinds + i]
        for t in range(2):
            base = (e * 2 + t) * tile
            at = slice((2 * i + t) * tile, (2 * i + t + 1) * tile)
            used = held > t * tile

            @pl.when(used)
            def _():
                pick = (info_rows[0:1, :] == slot + base).astype(F32).astype(BF)
                x = mm(pick, normed[...], NN).astype(BF)
                g = mm(pick, d_token[...], NN).astype(BF)
                hidden, slope = gelu_pair(mm(x, weight[0], NN))
                low = hidden.astype(BF)
                out_slots[at, :] = mm(low, weight[1], NT).astype(BF)
                d_pre = (mm(g, weight[1], NN) * slope).astype(BF)
                grad_slots[at, :] = mm(d_pre, weight[0], NT).astype(BF)
                d_in, d_out = mm(x, d_pre, TN), mm(g, low, TN)
                if t:
                    grad[0] += d_in
                    grad[1] += d_out
                else:
                    grad[0] = d_in
                    grad[1] = d_out

            @pl.when(jnp.logical_not(used))
            def _():
                out_slots[at, :] = jnp.zeros((tile, width), BF)
                grad_slots[at, :] = jnp.zeros((tile, width), BF)
                if not t:
                    grad[...] = jnp.zeros_like(grad)

        for k, out in enumerate(outs):
            place = owned_rows(k, chunk_count, out.shape[1])
            out[i] = grad[0, place, :].astype(BF)
            out[kinds + i] = grad[1, place, :].astype(BF)
    if last:
        total = jnp.zeros(gain_grad.shape, F32)
    column = lax.broadcasted_iota(jnp.int32, (rows, 2 * kinds * tile), 1) + chosen[0] * 2 * tile
    column = column.astype(F32)
    for k in range(4):
        at = slice(k * rows, (k + 1) * rows)
        pick = (info_cols[at, 0:1] == column).astype(F32).astype(BF)
        out = mm(pick, out_slots[...], NN)
        d_normed = mm(pick, grad_slots[...], NN)
        if not first:
            out += before[0][k].astype(F32)
            d_normed += before[1][k].astype(F32)
        if last:
            (out_send if k % 2 else out_keep)[k // 2] = out.astype(BF)
            wide = r_refs[k][...].astype(F32)
            inverse = rms_inverse(wide)
            unit = wide * inverse
            total += jnp.sum(d_normed * unit, axis=0, keepdims=True)
            (send if k % 2 else keep)[k // 2] = pullback(d_normed, unit, inverse, gain[...]).astype(BF)
        else:
            out_part[k] = out.astype(BF)
            grad_part[k] = d_normed.astype(BF)
    if last:
        gain_grad[...] = total


def moe_call(operands, chunks, chosen, first, last, shape, experts, capacity):
    rows, width, hidden = shape
    kinds, count = 2 * len(chosen), len(chunks)
    outs = []
    if first:
        outs += [shaped((4 * rows, width), BF)] * 2
    if last:
        outs += [shaped((2, rows, width), BF)] * 4 + [shaped((1, width), F32)]
    else:
        outs += [shaped((4, rows, width), BF)] * 2
    scratch = [
        pltpu.VMEM((2, width, hidden), BF),
        pltpu.VMEM((2, width, hidden), F32),
        pltpu.VMEM((len(chosen) * capacity, width), BF),
        pltpu.VMEM((len(chosen) * capacity, width), BF),
    ]
    return call(
        "moe_last" if last else "moe",
        functools.partial(moe_kernel, count, chosen, first, last, experts, capacity),
        outs + [shaped((kinds, width // count, hidden), BF)] * count,
        [*operands, *chunks],
        scratch,
        6e9 * len(chosen),
    )


def join_kernel(
    experts, x, a0, a1, a2, o0, o1, o2, s0, s1, s2, cotangent, gain, router, info_cols,
    output, d_resid, d_resid_low, small,
):
    def three(keep, got, across):
        return keep[0].astype(F32) + got[0].astype(F32) + across[...].astype(F32)

    rows = x.shape[0]
    residual = x[...].astype(F32) + three(a0, a1, a2)
    expert_own = three(o0, o1, o2)
    wide = residual.astype(BF).astype(F32)
    inverse = rms_inverse(wide)
    unit = wide * inverse
    low = (unit * gain[...]).astype(BF)
    probs, onehot, gate = route(low, router[...], info_cols[:rows, 1:2], experts)
    output[...] = (residual + gate * expert_own).astype(BF)
    cot = cotangent[...].astype(F32)
    d_gate = jnp.sum(cot * expert_own, axis=-1, keepdims=True)
    d_logits = d_gate * gate * (onehot - probs)
    d_rows = mm(d_logits, router[...].astype(F32), NT, HIGHEST)
    total = cot + three(s0, s1, s2) + pullback(d_rows, unit, inverse, gain[...])
    d_resid[...] = total
    d_resid_low[...] = total.astype(BF)
    small[0:8, :] = mm(d_logits, low.astype(F32), TN, HIGHEST)[:8]
    small[8:9, :] = jnp.sum(d_rows * unit, axis=0, keepdims=True)
    small[9:16, :] = jnp.zeros_like(small[9:16, :])


def call(name, kernel, outs, operands, scratch=(), flops=1e8, specs=None, out_specs=None):
    moved = sum(v.size * v.dtype.itemsize for v in operands)
    moved += sum(int(np.prod(s.shape)) * s.dtype.itemsize for s in outs)
    return pl.pallas_call(
        kernel,
        name=name,
        out_shape=outs,
        in_specs=specs or [VMEM] * len(operands),
        out_specs=out_specs or [VMEM] * len(outs),
        scratch_shapes=scratch,
        compiler_params=pltpu.CompilerParams(vmem_limit_bytes=VMEM_MIB.get(name, 60) * 2**20),
        cost_estimate=pl.CostEstimate(flops=int(flops), bytes_accessed=moved, transcendentals=0),
    )(*operands)


def shaped(shape, dtype):
    return jax.ShapeDtypeStruct(shape, dtype)


def body(
    layer_input, out_grad, attention_norm_scale, expert_norm_scale, query_weight, key_weight,
    value_weight, output_weight, bias_table, router_weight, expert_in, expert_out, expert_ids,
    slot_ids, piece_ids, bucket_table,
):
    rows, width = layer_input.shape
    size = lax.axis_size("dp")
    seq = rows * 4
    heads = query_weight.shape[1] // HEAD_DIM
    experts = expert_in.shape[0]
    hidden = expert_in.shape[2]
    capacity = 2 * seq // experts
    head_count, bucket_count = bias_table.shape
    ring = use_ring(size)
    local = heads * HEAD_DIM
    span = query_weight.shape[0]
    count = size if ring else 1
    held = width // count
    groups = GROUPS

    qkvo, *packed = call(
        "pack",
        functools.partial(pack_kernel, groups),
        [
            shaped((span, 4 * local), BF),
            *[shaped((2 * len(chosen), span, hidden), BF) for chosen in groups],
        ],
        [
            query_weight, key_weight, value_weight, output_weight, expert_in,
            jnp.transpose(expert_out, (0, 2, 1)),
        ],
    )
    x_pieces = tensor_gather(layer_input, "gather_input")
    if ring:
        qkvo_chunks = ring_gather(qkvo, size, size // 2, "gather_qkvo")
        packed = [tie(v, qkvo_chunks[3], qkvo_chunks[5]) for v in packed]
        group_chunks = [
            ring_gather(v, size, size // 2 - 1 + g % 2, f"gather_experts{g}")
            for g, v in enumerate(packed)
        ]
    else:
        qkvo_chunks = [lax.all_gather(qkvo, "dp", axis=0, tiled=True)]
        group_chunks = [[lax.all_gather(v, "dp", axis=1, tiled=True)] for v in packed]
    g_pieces = tensor_gather(out_grad, "gather_cotangent")
    buckets = jnp.pad(bucket_table, (0, 1), constant_values=-1).reshape(1, 2 * seq)
    info_rows, info_cols, wheel = call(
        "prepare", functools.partial(prepare_kernel, heads, experts, capacity),
        [shaped((8, seq), F32), shaped((seq, 8), F32), shaped((8, 2 * seq), F32)],
        [expert_ids.reshape(1, seq), piece_ids.reshape(1, seq), buckets, bias_table],
    )
    attn_gain = attention_norm_scale[None, :]
    moe_gain = expert_norm_scale[None, :]
    router = jnp.pad(router_weight, ((0, 0), (0, 128 - experts)))

    keep, send, normed_one, qkv, ctx, lse, weight = call(
        "attention_forward", functools.partial(attention_forward_kernel, count, heads),
        [
            shaped((2, rows, width), BF), shaped((2, rows, width), BF), shaped((seq, width), BF),
            shaped((seq, 768), BF), shaped((seq, 256), BF), shaped((seq, 128), F32),
            shaped((width, 1024), BF),
        ],
        [*x_pieces, attn_gain, wheel, info_rows, info_cols, *qkvo_chunks],
        [pltpu.VMEM((rows, 2 * seq), F32), pltpu.VMEM((4, rows, width), BF)],
        12e9,
    )
    if ring:
        send = tie(send, *(c[k] for c in group_chunks for k in (1, 7)), g_pieces[2])
    a_parts = tensor_scatter(keep, send, "sum_attention")
    resid_low = (
        layer_input.astype(F32)
        + (a_parts[0][0].astype(F32) + a_parts[1][0].astype(F32) + a_parts[2].astype(F32))
    ).astype(BF)
    r_pieces = tensor_gather(resid_low, "gather_residual")

    expert_grads, group_grads, rings = [], [], []
    for g, chosen in enumerate(groups):
        first, last = g == 0, g == len(groups) - 1
        operands = [*r_pieces, moe_gain, info_rows, info_cols]
        if first:
            operands += [*g_pieces, router]
        else:
            operands += [normed_two, d_token, out_part, grad_part]
        results = moe_call(
            operands, group_chunks[g], chosen, first, last, (rows, width, hidden), experts, capacity
        )
        if first:
            normed_two, d_token, results = results[0], results[1], results[2:]
        if last:
            out_keep, out_send, keep, send, moe_gain_grad, results = *results[:5], results[5:]
        else:
            out_part, grad_part, results = results[0], results[1], results[2:]
        if ring:
            hops = ring_scatter(results, size, size // 2 - 1 + g % 2, f"sum_grads{g}")
            next(hops)
            rings.append(hops)
            if first:
                early = hops.send(())
        else:
            total = lax.psum_scatter(results[0].astype(F32), "dp", scatter_dimension=1, tiled=True)
            expert_grads.append(total)
        group_grads.append(results)
    if ring:
        out_send, send = (tie(v, *early) for v in (out_send, send))
    o_parts = tensor_scatter(out_keep, out_send, "sum_experts")
    s_parts = tensor_scatter(keep, send, "sum_d_resid")
    if ring:
        wait = o_parts[1], s_parts[1]
        arrived = [hops.send(wait) for hops in rings]
        s_parts = *s_parts[:2], tie(s_parts[2], *arrived[0])

    layer_output, d_resid, d_resid_low, small = call(
        "join", functools.partial(join_kernel, experts),
        [
            shaped((rows, width), BF), shaped((rows, width), F32), shaped((rows, width), BF),
            shaped((16, width), F32),
        ],
        [
            layer_input, *a_parts, *o_parts, *s_parts,
            out_grad, moe_gain, router, info_cols,
        ],
        flops=1e9,
    )
    if ring:
        arrived[0] = rings[0].send(())
        d_resid_low = tie(d_resid_low, *arrived[1])
        arrived[1] = rings[1].send(())
    d_pieces = tensor_gather(d_resid_low, "gather_d_resid")
    if ring:
        wheel = tie(wheel, *arrived[0])
        arrived[0] = rings[0].send(())

    tiles = 7
    shared = [
        pltpu.VMEM((seq, 128), BF),
        pltpu.VMEM((128, seq), F32),
        pltpu.VMEM((seq, 128), F32),
        pltpu.VMEM((seq, 128), F32),
        pltpu.VMEM((seq, 128), F32),
        pltpu.VMEM((rows, 2 * seq), F32),
        pltpu.VMEM((tiles, rows, rows), F32),
        pltpu.VMEM((tiles, rows, rows), F32),
    ]
    operands = [*d_pieces, wheel, buckets, info_rows, info_cols, qkv, ctx, lse, weight]
    d_part, bias_grad = call(
        "attention_backward0",
        functools.partial(attention_backward_kernel, count, heads, 0),
        [shaped((seq, 384), BF), shaped((bucket_count, 128), F32)],
        operands,
        shared,
        12e9,
    )
    if ring:
        d_part = tie(d_part, *arrived[1], *arrived[0])
        arrived[1] = rings[1].send(())
    d_qkv, bias_grad, *qkvo_grads = call(
        "attention_backward1",
        functools.partial(attention_backward_kernel, count, heads, 1),
        [
            shaped((seq, 768), BF), shaped((bucket_count, 128), F32),
            *[shaped((held, 4 * local), BF)] * count,
        ],
        [*operands, normed_one, d_part, bias_grad],
        [pltpu.VMEM((width, 4 * local), F32), pltpu.VMEM((seq, width), BF), *shared],
        12e9,
    )
    if ring:
        hops = ring_scatter(qkvo_grads, size, size // 2, "sum_grads_qkvo")
        next(hops)
        for _ in range(size // 2):
            qkvo_up, qkvo_down = hops.send(())
    per = width // 128
    lines = (experts + 2) * per + bucket_count
    keep, send, sums = call(
        "input_share", functools.partial(input_share_kernel, experts),
        [
            shaped((2, rows, width), BF), shaped((2, rows, width), BF),
            shaped(((lines + 7) // 8 * 8, 128), F32),
        ],
        [*x_pieces, attn_gain, d_qkv, weight, small, moe_gain_grad, bias_grad],
        flops=2e9,
    )
    if ring:
        send = tie(send, *arrived[1])
        arrived[1] = rings[1].send(())
    i0, i1, i2 = tensor_scatter(keep, send, "sum_input_grad")
    input_grad = (
        d_resid + (i0[0].astype(F32) + i1[0].astype(F32) + i2.astype(F32))
    ).astype(BF)
    sums = sum_all(sums, size)
    grad_attn_gain = sums[:per].reshape(width)
    grad_moe_gain = sums[per : 2 * per].reshape(width)
    grad_router = jnp.transpose(sums[2 * per : (experts + 2) * per].reshape(experts, width))
    grad_bias_table = jnp.transpose(sums[(experts + 2) * per : lines, :head_count])

    if ring:
        qkvo_grad = (
            qkvo_grads[0].astype(F32) + qkvo_up.astype(F32) + qkvo_down.astype(F32)
        )
        grad_in, grad_out = call(
            "finish",
            functools.partial(finish_kernel, groups),
            [shaped((experts, span, hidden), F32)] * 2,
            [v for parts, came in zip(group_grads, arrived) for v in (parts[0], *came)],
        )
    else:
        qkvo_grad = lax.psum_scatter(
            qkvo_grads[0].astype(F32), "dp", scatter_dimension=0, tiled=True
        )
        kinds = [len(chosen) for chosen in groups]
        grad_in = jnp.concatenate([v[:n] for v, n in zip(expert_grads, kinds)], axis=0)
        grad_out = jnp.concatenate([v[n:] for v, n in zip(expert_grads, kinds)], axis=0)
    grad_query, grad_key, grad_value = (
        qkvo_grad[:, s * local : (s + 1) * local] for s in range(3)
    )
    grad_output = jnp.transpose(qkvo_grad[:, 3 * local :])
    grad_out = jnp.transpose(grad_out, (0, 2, 1))
    return (
        layer_output, input_grad, grad_attn_gain, grad_moe_gain, grad_query, grad_key, grad_value,
        grad_output, grad_bias_table, grad_router, grad_in, grad_out,
    )


def solution(mesh):
    in_specs = (
        P(("dp", "tensor"), None),
        P(("dp", "tensor"), None),
        P(),
        P(),
        P("dp", "tensor"),
        P("dp", "tensor"),
        P("dp", "tensor"),
        P("tensor", "dp"),
        P(),
        P(),
        P(None, "dp", "tensor"),
        P(None, "tensor", "dp"),
        P("dp"),
        P("dp"),
        P("dp"),
        P(),
    )
    out_specs = (
        P(("dp", "tensor"), None),
        P(("dp", "tensor"), None),
        P(),
        P(),
        P("dp", "tensor"),
        P("dp", "tensor"),
        P("dp", "tensor"),
        P("tensor", "dp"),
        P(),
        P(),
        P(None, "dp", "tensor"),
        P(None, "tensor", "dp"),
    )
    return jax.shard_map(body, mesh=mesh, in_specs=in_specs, out_specs=out_specs, check_vma=False)
```

```python
import functools

import jax
import jax.numpy as jnp
import numpy as np
from jax import lax
from jax.experimental import pallas as pl
from jax.experimental.pallas import tpu as pltpu
from jax.sharding import PartitionSpec as P

HEAD_DIM = 64
EPSILON = 1e-06
NEG_LARGE = -1e30
HIGHEST = lax.Precision.HIGHEST
BF = jnp.bfloat16
F32 = jnp.float32
NN = (((1,), (0,)), ((), ()))
NT = (((1,), (1,)), ((), ()))
TN = (((0,), (0,)), ((), ()))
VMEM = pl.BlockSpec(memory_space=pltpu.VMEM)
SMALL = 16
GROUPS = ((0, 1), (2, 3))
VMEM_MIB = {
    "pack": 4, "pack_experts": 8, "prepare": 12, "attention_forward": 28, "moe": 60, "moe_last": 60, "join": 14,
    "attention_backward0": 24, "attention_backward1": 28, "input_share": 16, "finish": 16,
}


def mm(left, right, dims, precision=None):
    return lax.dot_general(left, right, dims, preferred_element_type=F32, precision=precision)


def rms_inverse(rows):
    return lax.rsqrt(jnp.mean(rows * rows, axis=-1, keepdims=True) + EPSILON)


def pullback(grad, unit, inverse, gain):
    scaled = grad * gain
    return inverse * (scaled - unit * jnp.mean(scaled * unit, axis=-1, keepdims=True))


def tie(value, *others):
    if not others:
        return value
    return lax.optimization_barrier((value, *others))[0]


def ring_order(size):
    if size == 8:
        return (0, 2, 4, 6, 7, 5, 3, 1)
    return tuple(range(size))


def ring_perms(size):
    order = ring_order(size)
    ahead = [(order[i], order[(i + 1) % size]) for i in range(size)]
    return ahead, [(b, a) for a, b in ahead]


def use_ring(size):
    return size == 8


def ring_gather(chunk, size, far, name, waits=()):
    ahead, back = ring_perms(size)
    chunks = [chunk] + [None] * (size - 1)
    up = down = chunk
    for step in range(1, size):
        wait = waits[step - 1] if step <= len(waits) else ()
        if step <= far:
            with jax.named_scope(f"{name}_up{step}"):
                up = lax.ppermute(tie(up, *wait), "dp", ahead)
            chunks[size - step] = up
        if step <= size - 1 - far:
            with jax.named_scope(f"{name}_down{step}"):
                down = lax.ppermute(tie(down, *wait), "dp", back)
            chunks[step] = down
    return chunks


def add_low(left, right):
    return (left.astype(F32) + right.astype(F32)).astype(BF)


def ring_scatter(parts, size, far, name):
    ahead, back = ring_perms(size)
    near = size - 1 - far
    up, down = parts[far], parts[size - near]
    for step in range(max(far, near) + 1):
        wait = yield up, down
        if step < far:
            if step:
                up = add_low(up, parts[far - step])
            with jax.named_scope(f"{name}_up{step + 1}"):
                up = lax.ppermute(tie(up, *wait), "dp", ahead)
        if step < near:
            if step:
                down = add_low(down, parts[size - near + step])
            with jax.named_scope(f"{name}_down{step + 1}"):
                down = lax.ppermute(tie(down, *wait), "dp", back)


def tensor_perm(flip):
    return [(i, i ^ flip) for i in range(4)]


def swap(value, flip):
    return lax.ppermute(value, "tensor", tensor_perm(flip))


def tensor_gather(rows, name, late=True):
    with jax.named_scope(name):
        across = swap(rows, 2)
        beside = swap(rows, 1)
        return rows, beside, across, swap(across, 1)


def tensor_scatter(keep, send, name):
    with jax.named_scope(name):
        got = swap(send, 1)
        return keep, got, swap(add_low(keep[1::2], got[1::2]), 2)


def ring_rows(count, size):
    if count == 1:
        return [pl.ds(0, size)]
    me = lax.axis_index("dp")
    half = me >> 1
    place = jnp.where(me & 1 == 0, half, 7 - half)
    rows = []
    for k in range(count):
        at = (place + k) & 7
        owner = jnp.where(at < 4, 2 * at, 15 - 2 * at)
        rows.append(pl.ds(pl.multiple_of(owner * size, size), size))
    return rows


def pack_kernel(query, key, value, output, out):
    out[...] = jnp.concatenate(
        [query[...], key[...], value[...], jnp.transpose(output[...].astype(F32)).astype(BF)], axis=1
    )


def pack_experts_kernel(groups, w_in, w_out, *packed):
    for chosen, part in zip(groups, packed):
        for i, e in enumerate(chosen):
            part[i] = w_in[e]
            part[len(chosen) + i] = w_out[e]


def finish_kernel(groups, *refs):
    terms, (d_in, d_out) = refs[:-2], refs[-2:]
    for g, chosen in enumerate(groups):
        own, up, down = terms[3 * g : 3 * g + 3]
        for i in range(2 * len(chosen)):
            total = own[i].astype(F32) + up[i].astype(F32) + down[i].astype(F32)
            if i < len(chosen):
                d_in[chosen[i]] = total
            else:
                d_out[chosen[i - len(chosen)]] = total


def prepare_kernel(heads, experts, capacity, ids, pieces, buckets, table, rows, cols, wheel):
    seq = ids.shape[1]
    part = seq // 4
    me = lax.axis_index("tensor")
    seen = jnp.concatenate(
        [ids[:, pl.ds(pl.multiple_of((me ^ k) * part, part), part)] for k in range(4)], axis=1
    )
    chosen = lax.broadcasted_iota(jnp.int32, (8, seq), 0) == seen
    chosen = chosen.astype(F32)
    shape = (seq, seq)
    earlier = lax.broadcasted_iota(jnp.int32, shape, 0) < lax.broadcasted_iota(jnp.int32, shape, 1)
    rank = mm(chosen.astype(BF), earlier.astype(F32).astype(BF), NN)
    pos = jnp.sum(rank * chosen, axis=0, keepdims=True) + (seen * capacity).astype(F32)
    piece = pieces[...].astype(F32)
    held = jnp.concatenate(
        [pos, seen.astype(F32), jnp.where(piece > 0, piece, -1.0), jnp.zeros((5, seq), F32)], axis=0
    )
    rows[...] = held
    cols[...] = jnp.transpose(held)
    bucket = pltpu.roll(buckets[...], 2 * seq - (part - 1), 1)
    spread = lax.broadcasted_iota(jnp.int32, (table.shape[1], 2 * seq), 0) == bucket
    local = [table[pl.ds(me * heads + h, 1), :] for h in range(heads)]
    local.append(jnp.zeros((8 - heads, table.shape[1]), F32))
    wheel[...] = mm(jnp.concatenate(local, axis=0), spread.astype(F32), NN, HIGHEST)


def attention_forward_kernel(chunk_count, heads, *refs):
    x_refs, (gain, wheel, info_rows, info_cols) = refs[:4], refs[4:8]
    chunks = refs[8 : 8 + chunk_count]
    keep, send, qkv, ctx, lse, weight, bias, part, log_total = refs[8 + chunk_count :]
    rows = x_refs[0].shape[0]
    blocks = 4
    seq = rows * blocks
    me = lax.axis_index("tensor")
    width = heads * HEAD_DIM
    pad = 256
    for chunk, at in zip(chunks, ring_rows(chunk_count, chunks[0].shape[0])):
        size = chunk.shape[0]
        fill = jnp.zeros((size, pad - width), BF)
        whole = chunk[...]
        for s in range(4):
            weight[at, s * pad : (s + 1) * pad] = jnp.concatenate(
                [whole[:, s * width : (s + 1) * width], fill], axis=1
            )
    for k, x_ref in enumerate(x_refs):
        at = pl.ds(pl.multiple_of((me ^ k) * rows, rows), rows)
        wide = x_ref[...].astype(F32)
        low = (wide * rms_inverse(wide) * gain[...]).astype(BF)
        out = mm(low, weight[:, : 3 * pad], NN)
        qkv[at, :pad] = (out[:, :pad].astype(BF).astype(F32) * HEAD_DIM**-0.5).astype(BF)
        qkv[at, pad:] = out[:, pad:].astype(BF)
    lane = lax.broadcasted_iota(jnp.int32, (rows, 128), 1)
    ctx[...] = jnp.zeros_like(ctx)
    log_total[...] = jnp.zeros_like(log_total)

    def head_step(head, carry):
        pair = pl.multiple_of((head // 2) * 128, 128)
        mine = lane // HEAD_DIM == head % 2
        bias[...] = pltpu.roll(
            jnp.broadcast_to(wheel[pl.ds(head, 1), :], (rows, 2 * seq)), 0, 1, stride=1, stride_axis=0
        )
        for b in range(blocks):
            at = slice(b * rows, (b + 1) * rows)
            keys = min(b + 2, blocks) * rows
            q = jnp.where(mine, qkv[at, pl.ds(pair, 128)], jnp.zeros((), BF))
            k = qkv[:keys, pl.ds(pad + pair, 128)]
            v = qkv[:keys, pl.ds(2 * pad + pair, 128)]
            start = (blocks - 1 - b) * rows
            scores = mm(q, k, NT) + bias[:, start : start + keys]
            pieces = []
            if b:
                pieces.append(scores[:, : b * rows])
            tail = scores[:, b * rows :]
            shape = tail.shape
            piece = info_cols[at, 2:3]
            kept = (piece == info_rows[2:3, b * rows : keys]) & (piece > 0)
            kept = kept | (
                lax.broadcasted_iota(jnp.int32, shape, 1)
                <= lax.broadcasted_iota(jnp.int32, shape, 0)
            )
            pieces.append(jnp.where(kept, tail, NEG_LARGE))
            scores = jnp.concatenate(pieces, axis=1) if b else pieces[0]
            peak = jnp.max(scores, axis=-1, keepdims=True)
            prob = jnp.exp(scores - peak)
            total = jnp.sum(prob, axis=-1, keepdims=True)
            out = mm(prob.astype(BF), v, NN) / total
            ctx[at, pl.ds(pair, 128)] = jnp.where(mine, out.astype(BF), ctx[at, pl.ds(pair, 128)])
            log_total[at, :] = jnp.where(lane == head, peak + jnp.log(total), log_total[at, :])
        return carry

    lax.fori_loop(0, heads, head_step, 0)
    lse[...] = jnp.transpose(log_total[...])[:8]
    for b in range(blocks):
        part[me ^ b] = mm(ctx[b * rows : (b + 1) * rows, :], weight[:, 3 * pad :], NT).astype(BF)
    for k in range(2):
        keep[k] = part[2 * k]
        send[k] = part[2 * k + 1]


def attention_backward_kernel(owner_count, heads, pair_index, *refs):
    last = pair_index == 1
    d_refs, (wheel, buckets, info_rows, info_cols, qkv, ctx, lse, weight) = refs[:4], refs[4:12]
    refs = refs[12:]
    if last:
        x_refs, (gain, before, bias_before, d_qkv, bias_grad), refs = refs[:4], refs[4:9], refs[9:]
        outs, refs = refs[:owner_count], refs[owner_count:]
        grad, d_resid, normed, refs = *refs[:3], refs[3:]
    else:
        d_part, bias_grad, refs = refs[0], refs[1], refs[2:]
    d_ctx, d_q, d_k, d_v, slope, bias, d_bias = refs
    rows = d_refs[0].shape[0]
    blocks = 4
    seq = rows * blocks
    me = lax.axis_index("tensor")
    width = heads * HEAD_DIM
    pad = 256
    tiles = 2 * blocks - 1
    pair = 128 * pair_index
    here = slice(pair, pair + 128)
    for k, d_ref in enumerate(d_refs):
        at = pl.ds(pl.multiple_of((me ^ k) * rows, rows), rows)
        low = d_ref[...]
        if last:
            d_resid[at, :] = low
            wide = x_refs[k][...].astype(F32)
            normed[at, :] = (wide * rms_inverse(wide) * gain[...]).astype(BF)
        d_ctx[at, :] = mm(low, weight[:, 3 * pad + pair : 3 * pad + pair + 128], NN).astype(BF)
    lane = lax.broadcasted_iota(jnp.int32, (rows, 128), 1)
    d_q[...] = jnp.zeros_like(d_q)
    d_k[...] = jnp.zeros_like(d_k)
    d_v[...] = jnp.zeros_like(d_v)
    bias_grad[...] = bias_before[...] if last else jnp.zeros_like(bias_grad)
    none = jnp.zeros((), BF)
    bucket = pltpu.roll(buckets[...], 2 * seq - (rows - 1), 1)
    spread = lax.broadcasted_iota(jnp.int32, (bias_grad.shape[0], 2 * seq), 0) == bucket
    head_lane = lax.broadcasted_iota(jnp.int32, bias_grad.shape, 1)

    def head_step(head, carry):
        mine = lane // HEAD_DIM == head % 2
        slope[...] = pltpu.roll(
            jnp.broadcast_to(wheel[pl.ds(head, 1), :], (rows, 2 * seq)), 0, 1, stride=1, stride_axis=0
        )
        for a in range(tiles):
            bias[a] = jnp.transpose(slope[:, a * rows : (a + 1) * rows])
        d_bias[...] = jnp.zeros_like(d_bias)
        for b in range(blocks):
            at = slice(b * rows, (b + 1) * rows)
            q = jnp.where(mine, qkv[at, here], none)
            g = jnp.where(mine, d_ctx[at, :], none)
            base = jnp.sum(
                jnp.transpose(g.astype(F32) * ctx[at, here].astype(F32)), axis=0, keepdims=True
            )
            log_total = lse[pl.ds(head, 1), at]
            d_q_block = jnp.zeros((rows, 128), F32)
            for t in range(min(b + 2, blocks)):
                over = slice(t * rows, (t + 1) * rows)
                a = t - b + blocks - 1
                k = qkv[over, pad + pair : pad + pair + 128]
                scores = mm(k, q, NT) + bias[a]
                prob = jnp.exp(scores - log_total)
                if t >= b:
                    piece = info_cols[over, 2:3]
                    kept = (piece == info_rows[2:3, at]) & (piece > 0)
                    if t == b:
                        shape = (rows, rows)
                        kept = kept | (
                            lax.broadcasted_iota(jnp.int32, shape, 0)
                            <= lax.broadcasted_iota(jnp.int32, shape, 1)
                        )
                    prob = jnp.where(kept, prob, 0.0)
                d_v[over, :] += mm(prob.astype(BF), g, NN)
                d_prob = mm(qkv[over, 2 * pad + pair : 2 * pad + pair + 128], g, NT)
                d_score = (prob * (d_prob - base)).astype(BF)
                d_bias[a] += d_score.astype(F32)
                d_k[over, :] += mm(d_score, q, NN)
                d_q_block += mm(d_score, k, TN)
            d_q[at, :] += jnp.where(mine, d_q_block, 0.0)
        for a in range(tiles):
            slope[:, a * rows : (a + 1) * rows] = jnp.transpose(d_bias[a])
        slope[:, tiles * rows :] = jnp.zeros((rows, rows), F32)
        total = jnp.zeros((8, 2 * seq), F32)
        for g8 in range(rows // 8):
            total += pltpu.roll(slope[g8 * 8 : g8 * 8 + 8, :], (2 * seq - g8 * 8) % (2 * seq), 1)
        line = total[0:1]
        for s in range(1, 8):
            line += pltpu.roll(total, 2 * seq - s, 1)[s : s + 1]
        column = jnp.sum(jnp.where(spread, line, 0.0), axis=1, keepdims=True)
        bias_grad[...] = jnp.where(head_lane == me * heads + head, column, bias_grad[...])
        return carry

    lax.fori_loop(2 * pair_index, min(heads, 2 * pair_index + 2), head_step, 0)
    for s, value in enumerate((d_q[...] * HEAD_DIM**-0.5, d_k[...], d_v[...])):
        if last:
            d_qkv[:, s * pad : s * pad + pair] = before[:, s * 128 : (s + 1) * 128]
            d_qkv[:, s * pad + pair : (s + 1) * pad] = value.astype(BF)
        else:
            d_part[:, s * 128 : (s + 1) * 128] = value.astype(BF)
    if not last:
        return
    for s in range(3):
        out = mm(normed[...], d_qkv[:, s * pad : (s + 1) * pad], TN)
        grad[:, s * width : (s + 1) * width] = out[:, :width]
    grad[:, 3 * width :] = mm(d_resid[...], ctx[...], TN)[:, :width]
    span = grad.shape[0] // owner_count
    for out, at in zip(outs, ring_rows(owner_count, span)):
        out[:span, :] = grad[at, :].astype(BF)
        if out.shape[0] > span:
            out[span:, :] = jnp.zeros((out.shape[0] - span, out.shape[1]), BF)


def input_share_kernel(experts, *refs):
    x_refs = refs[:4]
    gain, d_qkv, weight, small, moe_gain_grad, bias_grad, keep, send, sums = refs[4:]
    rows, width = x_refs[0].shape
    me = lax.axis_index("tensor")
    total = jnp.zeros((1, width), F32)
    for k, x_ref in enumerate(x_refs):
        at = pl.ds(pl.multiple_of((me ^ k) * rows, rows), rows)
        wide = x_ref[...].astype(F32)
        inverse = rms_inverse(wide)
        unit = wide * inverse
        d_normed = mm(d_qkv[at, :], weight[:, :768], NT)
        total += jnp.sum(d_normed * unit, axis=0, keepdims=True)
        share = pullback(d_normed, unit, inverse, gain[...]).astype(BF)
        (send if k % 2 else keep)[k // 2] = share
    lines = [total, moe_gain_grad[...] + small[8:9, :]] + [small[e : e + 1, :] for e in range(experts)]
    sums[...] = jnp.zeros_like(sums)
    for i, line in enumerate(lines):
        sums[i : i + 1, :] = line
    for i in range(bias_grad.shape[0] // 8):
        sums[8:16, i * 128 : (i + 1) * 128] = bias_grad[i * 8 : i * 8 + 8, :]


def gelu_pair(u):
    c = float(np.sqrt(2.0 / np.pi))
    square = u * u
    t = jnp.tanh(c * u * (1.0 + 0.044715 * square))
    half = 0.5 * (1.0 + t)
    slope = half + 0.5 * c * u * (1.0 - t * t) * (1.0 + 3 * 0.044715 * square)
    return u * half, slope


def route(low, router, expert_col, experts):
    logits = mm(low, router, NN)
    lane = lax.broadcasted_iota(jnp.int32, logits.shape, 1)
    logits = jnp.where(lane < experts, logits, NEG_LARGE)
    grown = jnp.exp(logits - jnp.max(logits, axis=-1, keepdims=True))
    probs = grown / jnp.sum(grown, axis=-1, keepdims=True)
    onehot = (lane == expert_col).astype(F32)
    return probs, onehot, jnp.sum(probs * onehot, axis=-1, keepdims=True)


def moe_kernel(chunk_count, chosen, first, last, experts, capacity, *refs):
    kinds = len(chosen)
    r_refs, refs = refs[:4], refs[4:]
    gain, info_rows, info_cols, refs = refs[0], refs[1], refs[2], refs[3:]
    if first:
        g_refs, router, refs = refs[:4], refs[4], refs[5:]
    else:
        normed, d_token, before, refs = refs[0], refs[1], refs[2:4], refs[4:]
    chunks, refs = refs[:chunk_count], refs[chunk_count:]
    if first:
        normed, d_token, refs = refs[0], refs[1], refs[2:]
    if last:
        keep, send, gain_grad, refs = *refs[:3], refs[3:]
    else:
        out_part, grad_part, refs = refs[0], refs[1], refs[2:]
    outs, refs = refs[:chunk_count], refs[chunk_count:]
    weight, grad, out_slots, grad_slots = refs
    rows, width = r_refs[0].shape
    seq = 4 * rows
    tile = capacity // 2
    if first:
        for k in range(4):
            at = slice(k * rows, (k + 1) * rows)
            wide = r_refs[k][...].astype(F32)
            low = (wide * rms_inverse(wide) * gain[...]).astype(BF)
            normed[at, :] = low
            gate = route(low, router[...], info_cols[at, 1:2], experts)[2]
            d_token[at, :] = (gate * g_refs[k][...].astype(F32)).astype(BF)
    places = ring_rows(chunk_count, chunks[0].shape[1])
    slot = lax.broadcasted_iota(jnp.int32, (tile, seq), 0).astype(F32)
    for i, e in enumerate(chosen):
        held = jnp.sum((info_rows[1:2, :] == e).astype(F32))
        for chunk, place in zip(chunks, places):
            weight[0, place, :] = chunk[i]
            weight[1, place, :] = chunk[kinds + i]
        for t in range(2):
            base = (e * 2 + t) * tile
            at = slice((2 * i + t) * tile, (2 * i + t + 1) * tile)
            used = held > t * tile

            @pl.when(used)
            def _():
                pick = (info_rows[0:1, :] == slot + base).astype(F32).astype(BF)
                x = mm(pick, normed[...], NN).astype(BF)
                g = mm(pick, d_token[...], NN).astype(BF)
                hidden, slope = gelu_pair(mm(x, weight[0], NN))
                low = hidden.astype(BF)
                out_slots[at, :] = mm(low, weight[1], NT).astype(BF)
                d_pre = (mm(g, weight[1], NN) * slope).astype(BF)
                grad_slots[at, :] = mm(d_pre, weight[0], NT).astype(BF)
                d_in, d_out = mm(x, d_pre, TN), mm(g, low, TN)
                if t:
                    grad[0] += d_in
                    grad[1] += d_out
                else:
                    grad[0] = d_in
                    grad[1] = d_out

            @pl.when(jnp.logical_not(used))
            def _():
                out_slots[at, :] = jnp.zeros((tile, width), BF)
                grad_slots[at, :] = jnp.zeros((tile, width), BF)
                if not t:
                    grad[...] = jnp.zeros_like(grad)

        for out, place in zip(outs, places):
            out[i] = grad[0, place, :].astype(BF)
            out[kinds + i] = grad[1, place, :].astype(BF)
    if last:
        total = jnp.zeros(gain_grad.shape, F32)
    column = lax.broadcasted_iota(jnp.int32, (rows, 2 * kinds * tile), 1) + chosen[0] * 2 * tile
    column = column.astype(F32)
    for k in range(4):
        at = slice(k * rows, (k + 1) * rows)
        pick = (info_cols[at, 0:1] == column).astype(F32).astype(BF)
        out = mm(pick, out_slots[...], NN)
        d_normed = mm(pick, grad_slots[...], NN)
        if not first:
            out += before[0][k].astype(F32)
            d_normed += before[1][k].astype(F32)
        if last:
            (send if k % 2 else keep)[k // 2] = out.astype(BF)
            wide = r_refs[k][...].astype(F32)
            inverse = rms_inverse(wide)
            unit = wide * inverse
            total += jnp.sum(d_normed * unit, axis=0, keepdims=True)
            (send if k % 2 else keep)[2 + k // 2] = pullback(
                d_normed, unit, inverse, gain[...]
            ).astype(BF)
        else:
            out_part[k] = out.astype(BF)
            grad_part[k] = d_normed.astype(BF)
    if last:
        gain_grad[...] = total


def moe_call(operands, chunks, chosen, first, last, shape, experts, capacity):
    rows, width, hidden = shape
    kinds, count = 2 * len(chosen), len(chunks)
    outs = []
    if first:
        outs += [shaped((4 * rows, width), BF)] * 2
    if last:
        outs += [shaped((4, rows, width), BF)] * 2 + [shaped((1, width), F32)]
    else:
        outs += [shaped((4, rows, width), BF)] * 2
    scratch = [
        pltpu.VMEM((2, width, hidden), BF),
        pltpu.VMEM((2, width, hidden), F32),
        pltpu.VMEM((len(chosen) * capacity, width), BF),
        pltpu.VMEM((len(chosen) * capacity, width), BF),
    ]
    return call(
        "moe_last" if last else "moe",
        functools.partial(moe_kernel, count, chosen, first, last, experts, capacity),
        outs + [shaped((kinds, width // count, hidden), BF)] * count,
        [*operands, *chunks],
        scratch,
        6e9 * len(chosen),
    )


def join_kernel(
    experts, x, a0, a1, a2, m0, m1, m2, cotangent, gain, router, info_cols,
    output, d_resid, d_resid_low, small,
):
    def three(keep, got, across, n):
        return keep[2 * n].astype(F32) + got[2 * n].astype(F32) + across[n].astype(F32)

    rows = x.shape[0]
    residual = x[...].astype(F32) + three(a0, a1, a2, 0)
    expert_own = three(m0, m1, m2, 0)
    wide = residual.astype(BF).astype(F32)
    inverse = rms_inverse(wide)
    unit = wide * inverse
    low = (unit * gain[...]).astype(BF)
    probs, onehot, gate = route(low, router[...], info_cols[:rows, 1:2], experts)
    output[...] = (residual + gate * expert_own).astype(BF)
    cot = cotangent[...].astype(F32)
    d_gate = jnp.sum(cot * expert_own, axis=-1, keepdims=True)
    d_logits = d_gate * gate * (onehot - probs)
    d_rows = mm(d_logits, router[...].astype(F32), NT, HIGHEST)
    total = cot + three(m0, m1, m2, 1) + pullback(d_rows, unit, inverse, gain[...])
    d_resid[...] = total
    d_resid_low[...] = total.astype(BF)
    small[0:8, :] = mm(d_logits, low.astype(F32), TN, HIGHEST)[:8]
    small[8:9, :] = jnp.sum(d_rows * unit, axis=0, keepdims=True)
    small[9:16, :] = jnp.zeros_like(small[9:16, :])


def call(name, kernel, outs, operands, scratch=(), flops=1e8, specs=None, out_specs=None):
    moved = sum(v.size * v.dtype.itemsize for v in operands)
    moved += sum(int(np.prod(s.shape)) * s.dtype.itemsize for s in outs)
    return pl.pallas_call(
        kernel,
        name=name,
        out_shape=outs,
        in_specs=specs or [VMEM] * len(operands),
        out_specs=out_specs or [VMEM] * len(outs),
        scratch_shapes=scratch,
        compiler_params=pltpu.CompilerParams(vmem_limit_bytes=VMEM_MIB.get(name, 60) * 2**20),
        cost_estimate=pl.CostEstimate(flops=int(flops), bytes_accessed=moved, transcendentals=0),
    )(*operands)


def shaped(shape, dtype):
    return jax.ShapeDtypeStruct(shape, dtype)


def body(
    layer_input, out_grad, attention_norm_scale, expert_norm_scale, query_weight, key_weight,
    value_weight, output_weight, bias_table, router_weight, expert_in, expert_out, expert_ids,
    slot_ids, piece_ids, bucket_table,
):
    rows, width = layer_input.shape
    size = lax.axis_size("dp")
    seq = rows * 4
    heads = query_weight.shape[1] // HEAD_DIM
    experts = expert_in.shape[0]
    hidden = expert_in.shape[2]
    capacity = 2 * seq // experts
    head_count, bucket_count = bias_table.shape
    ring = use_ring(size)
    local = heads * HEAD_DIM
    span = query_weight.shape[0]
    count = size if ring else 1
    held = width // count
    groups = GROUPS

    (qkvo,) = call(
        "pack",
        pack_kernel,
        [shaped((span, 4 * local), BF)],
        [query_weight, key_weight, value_weight, output_weight],
    )
    packed = call(
        "pack_experts",
        functools.partial(pack_experts_kernel, groups),
        [shaped((2 * len(chosen), span, hidden), BF) for chosen in groups],
        [expert_in, jnp.transpose(expert_out, (0, 2, 1))],
    )
    buckets = jnp.pad(bucket_table, (0, 1), constant_values=-1).reshape(1, 2 * seq)
    info_rows, info_cols, wheel = call(
        "prepare",
        functools.partial(prepare_kernel, heads, experts, capacity),
        [shaped((8, seq), F32), shaped((seq, 8), F32), shaped((8, 2 * seq), F32)],
        [expert_ids.reshape(1, seq), piece_ids.reshape(1, seq), buckets, bias_table],
    )
    x_pieces = tensor_gather(layer_input, "gather_input", late=False)
    if ring:
        qkvo_chunks = ring_gather(
            qkvo, size, size // 2, "gather_qkvo", ((), tuple(packed), (info_rows, info_cols, wheel))
        )
        packed = [tie(v, qkvo_chunks[3], qkvo_chunks[5]) for v in packed]
        group_chunks = [
            ring_gather(v, size, size // 2 - 1 + g % 2, f"gather_experts{g}")
            for g, v in enumerate(packed)
        ]
    else:
        qkvo_chunks = [lax.all_gather(qkvo, "dp", axis=0, tiled=True)]
        group_chunks = [[lax.all_gather(v, "dp", axis=1, tiled=True)] for v in packed]
    g_pieces = tensor_gather(out_grad, "gather_cotangent")
    attn_gain = attention_norm_scale[None, :]
    moe_gain = expert_norm_scale[None, :]
    router = jnp.pad(router_weight, ((0, 0), (0, 128 - experts)))

    keep, send, qkv, ctx, lse, weight = call(
        "attention_forward", functools.partial(attention_forward_kernel, count, heads),
        [
            shaped((2, rows, width), BF), shaped((2, rows, width), BF), shaped((seq, 768), BF),
            shaped((seq, 256), BF), shaped((8, seq), F32), shaped((width, 1024), BF),
        ],
        [*x_pieces, attn_gain, wheel, info_rows, info_cols, *qkvo_chunks],
        [
            pltpu.VMEM((rows, 2 * seq), F32),
            pltpu.VMEM((4, rows, width), BF),
            pltpu.VMEM((seq, 128), F32),
        ],
        12e9,
    )
    if ring:
        send = tie(send, group_chunks[0][1], group_chunks[0][7], g_pieces[2])
    wait = (group_chunks[1][1], group_chunks[1][7]) if ring else ()
    a_parts = tensor_scatter(keep, send, "sum_attention")
    a_parts = (*a_parts[:2], tie(a_parts[2], *wait))
    resid_low = (
        layer_input.astype(F32)
        + (a_parts[0][0].astype(F32) + a_parts[1][0].astype(F32) + a_parts[2][0].astype(F32))
    ).astype(BF)
    if ring:
        resid_low = tie(resid_low, group_chunks[0][2], group_chunks[0][6])
    r_pieces = tensor_gather(resid_low, "gather_residual")

    expert_grads, group_grads, rings = [], [], []
    for g, chosen in enumerate(groups):
        first, last = g == 0, g == len(groups) - 1
        operands = [*r_pieces, moe_gain, info_rows, info_cols]
        if first:
            operands += [*g_pieces, router]
        else:
            operands += [normed_two, d_token, out_part, grad_part]
        results = moe_call(
            operands, group_chunks[g], chosen, first, last, (rows, width, hidden), experts, capacity
        )
        if first:
            normed_two, d_token, results = results[0], results[1], results[2:]
        if last:
            keep, send, moe_gain_grad, results = *results[:3], results[3:]
        else:
            out_part, grad_part, results = results[0], results[1], results[2:]
        if ring:
            hops = ring_scatter(results, size, size // 2 - 1 + g % 2, f"sum_grads{g}")
            next(hops)
            rings.append(hops)
            if first:
                early = hops.send(())
        else:
            total = lax.psum_scatter(results[0].astype(F32), "dp", scatter_dimension=1, tiled=True)
            expert_grads.append(total)
        group_grads.append(results)
    if ring:
        send = tie(send, *early)
    m_parts = tensor_scatter(keep, send, "sum_experts_d_resid")
    if ring:
        wait = (m_parts[1],)
        arrived = [hops.send(wait) for hops in rings]

    layer_output, d_resid, d_resid_low, small = call(
        "join", functools.partial(join_kernel, experts),
        [
            shaped((rows, width), BF), shaped((rows, width), F32), shaped((rows, width), BF),
            shaped((16, width), F32),
        ],
        [
            layer_input, *a_parts, *m_parts,
            out_grad, moe_gain, router, info_cols,
        ],
        flops=1e9,
    )
    if ring:
        arrived[0] = rings[0].send(())
    d_pieces = tensor_gather(d_resid_low, "gather_d_resid")
    if ring:
        wheel = tie(wheel, *arrived[1])
        arrived[1] = rings[1].send(())

    tiles = 7
    shared = [
        pltpu.VMEM((seq, 128), BF),
        pltpu.VMEM((seq, 128), F32),
        pltpu.VMEM((seq, 128), F32),
        pltpu.VMEM((seq, 128), F32),
        pltpu.VMEM((rows, 2 * seq), F32),
        pltpu.VMEM((tiles, rows, rows), F32),
        pltpu.VMEM((tiles, rows, rows), F32),
    ]
    operands = [*d_pieces, wheel, buckets, info_rows, info_cols, qkv, ctx, lse, weight]
    d_part, bias_grad = call(
        "attention_backward0",
        functools.partial(attention_backward_kernel, count, heads, 0),
        [shaped((seq, 384), BF), shaped((bucket_count, 128), F32)],
        operands,
        shared,
        12e9,
    )
    if ring:
        wait = (d_part,)
        d_part = tie(d_part, *arrived[0])
        arrived[0] = rings[0].send(wait)
    d_qkv, bias_grad, *qkvo_grads = call(
        "attention_backward1",
        functools.partial(attention_backward_kernel, count, heads, 1),
        [
            shaped((seq, 768), BF), shaped((bucket_count, 128), F32),
            *[shaped((held + SMALL * ring, 4 * local), BF)] * count,
        ],
        [*operands, *x_pieces, attn_gain, d_part, bias_grad],
        [
            pltpu.VMEM((width, 4 * local), F32),
            pltpu.VMEM((seq, width), BF),
            pltpu.VMEM((seq, width), BF),
            *shared,
        ],
        12e9,
    )
    if ring:
        wait = (d_qkv,)
        d_qkv = tie(d_qkv, *arrived[1], *arrived[0])
        arrived[1] = rings[1].send(wait)
    keep, send, sums = call(
        "input_share", functools.partial(input_share_kernel, experts),
        [
            shaped((2, rows, width), BF), shaped((2, rows, width), BF), shaped((SMALL, width), F32),
        ],
        [*x_pieces, attn_gain, d_qkv, weight, small, moe_gain_grad, bias_grad],
        flops=2e9,
    )
    if ring:
        arrived[1] = rings[1].send(())
    i0, i1, i2 = tensor_scatter(keep, send, "sum_input_grad")
    input_grad = (
        d_resid + (i0[0].astype(F32) + i1[0].astype(F32) + i2[0].astype(F32))
    ).astype(BF)
    if ring:
        own = jnp.pad(sums.astype(BF), ((held, 0), (0, 0)))
        sent = [v + own if k in (3, 4) else v for k, v in enumerate(qkvo_grads)]
        hops = ring_scatter(sent, size, 3, "sum_grads_qkvo")
        next(hops)
        sums = own[held:].astype(F32)
        for hop in range(4):
            qkvo_up, qkvo_down = hops.send((i1,) if hop == 1 else ())
            sums = sums + qkvo_down[held:].astype(F32)
            if hop < 3:
                sums = sums + qkvo_up[held:].astype(F32)
    else:
        sums = lax.psum(sums, "dp")
    sums = sums + swap(sums, 1)
    sums = sums + swap(sums, 2)
    grad_attn_gain, grad_moe_gain = sums[0], sums[1]
    grad_router = jnp.transpose(sums[2 : 2 + experts])
    grad_bias_table = jnp.transpose(
        jnp.concatenate(
            [sums[8:16, i * 128 : i * 128 + head_count] for i in range(bucket_count // 8)], axis=0
        )
    )
    if ring:
        qkvo_grad = (
            qkvo_grads[0].astype(F32) + qkvo_up.astype(F32) + qkvo_down.astype(F32)
        )[:held]
        group_grads[0] = [tie(group_grads[0][0], qkvo_up, qkvo_down)]
        grad_in, grad_out = call(
            "finish",
            functools.partial(finish_kernel, groups),
            [shaped((experts, span, hidden), F32)] * 2,
            [v for parts, came in zip(group_grads, arrived) for v in (parts[0], *came)],
        )
    else:
        qkvo_grad = lax.psum_scatter(
            qkvo_grads[0].astype(F32), "dp", scatter_dimension=0, tiled=True
        )
        kinds = [len(chosen) for chosen in groups]
        grad_in = jnp.concatenate([v[:n] for v, n in zip(expert_grads, kinds)], axis=0)
        grad_out = jnp.concatenate([v[n:] for v, n in zip(expert_grads, kinds)], axis=0)
    grad_query, grad_key, grad_value = (
        qkvo_grad[:, s * local : (s + 1) * local] for s in range(3)
    )
    grad_output = jnp.transpose(qkvo_grad[:, 3 * local :])
    grad_out = jnp.transpose(grad_out, (0, 2, 1))
    return (
        layer_output, input_grad, grad_attn_gain, grad_moe_gain, grad_query, grad_key, grad_value,
        grad_output, grad_bias_table, grad_router, grad_in, grad_out,
    )


def solution(mesh):
    in_specs = (
        P(("dp", "tensor"), None),
        P(("dp", "tensor"), None),
        P(),
        P(),
        P("dp", "tensor"),
        P("dp", "tensor"),
        P("dp", "tensor"),
        P("tensor", "dp"),
        P(),
        P(),
        P(None, "dp", "tensor"),
        P(None, "tensor", "dp"),
        P("dp"),
        P("dp"),
        P("dp"),
        P(),
    )
    out_specs = (
        P(("dp", "tensor"), None),
        P(("dp", "tensor"), None),
        P(),
        P(),
        P("dp", "tensor"),
        P("dp", "tensor"),
        P("dp", "tensor"),
        P("tensor", "dp"),
        P(),
        P(),
        P(None, "dp", "tensor"),
        P(None, "tensor", "dp"),
    )
    return jax.shard_map(body, mesh=mesh, in_specs=in_specs, out_specs=out_specs, check_vma=False)
```

```python
import functools

import jax
import jax.numpy as jnp
import numpy as np
from jax import lax
from jax.experimental import pallas as pl
from jax.experimental.pallas import tpu as pltpu
from jax.sharding import PartitionSpec as P

HEAD_DIM = 64
EPSILON = 1e-06
NEG_LARGE = -1e30
HIGHEST = lax.Precision.HIGHEST
BF = jnp.bfloat16
F32 = jnp.float32
NN = (((1,), (0,)), ((), ()))
NT = (((1,), (1,)), ((), ()))
TN = (((0,), (0,)), ((), ()))
VMEM = pl.BlockSpec(memory_space=pltpu.VMEM)
SMALL = 16
GROUPS = ((0, 1), (2, 3))
VMEM_MIB = {
    "pack": 4, "pack_experts": 8, "prepare": 12, "attention_forward": 28, "moe": 60, "moe_last": 60, "join": 14,
    "attention_backward0": 24, "attention_backward1": 28, "input_share": 16, "finish": 16,
}


def mm(left, right, dims, precision=None):
    return lax.dot_general(left, right, dims, preferred_element_type=F32, precision=precision)


def rms_inverse(rows):
    return lax.rsqrt(jnp.mean(rows * rows, axis=-1, keepdims=True) + EPSILON)


def pullback(grad, unit, inverse, gain):
    scaled = grad * gain
    return inverse * (scaled - unit * jnp.mean(scaled * unit, axis=-1, keepdims=True))


def tie(value, *others):
    if not others:
        return value
    return lax.optimization_barrier((value, *others))[0]


def ring_order(size):
    if size == 8:
        return (0, 2, 4, 6, 7, 5, 3, 1)
    return tuple(range(size))


def ring_perms(size):
    order = ring_order(size)
    ahead = [(order[i], order[(i + 1) % size]) for i in range(size)]
    return ahead, [(b, a) for a, b in ahead]


def use_ring(size):
    return size == 8


def ring_gather(chunk, size, far, name, waits=()):
    ahead, back = ring_perms(size)
    chunks = [chunk] + [None] * (size - 1)
    up = down = chunk
    for step in range(1, size):
        wait = waits[step - 1] if step <= len(waits) else ()
        if step <= far:
            with jax.named_scope(f"{name}_up{step}"):
                up = lax.ppermute(tie(up, *wait), "dp", ahead)
            chunks[size - step] = up
        if step <= size - 1 - far:
            with jax.named_scope(f"{name}_down{step}"):
                down = lax.ppermute(tie(down, *wait), "dp", back)
            chunks[step] = down
    return chunks


def add_low(left, right):
    return (left.astype(F32) + right.astype(F32)).astype(BF)


def ring_scatter(parts, size, far, name):
    ahead, back = ring_perms(size)
    near = size - 1 - far
    up, down = parts[far], parts[size - near]
    for step in range(max(far, near) + 1):
        wait = yield up, down
        if step < far:
            if step:
                up = add_low(up, parts[far - step])
            with jax.named_scope(f"{name}_up{step + 1}"):
                up = lax.ppermute(tie(up, *wait), "dp", ahead)
        if step < near:
            if step:
                down = add_low(down, parts[size - near + step])
            with jax.named_scope(f"{name}_down{step + 1}"):
                down = lax.ppermute(tie(down, *wait), "dp", back)


def tensor_perm(flip):
    return [(i, i ^ flip) for i in range(4)]


def swap(value, flip):
    return lax.ppermute(value, "tensor", tensor_perm(flip))


def tensor_gather(rows, name, late=True):
    with jax.named_scope(name):
        across = swap(rows, 2)
        beside = swap(rows, 1)
        return rows, beside, across, swap(across, 1)


def tensor_scatter(keep, send, name):
    with jax.named_scope(name):
        got = swap(send, 1)
        return keep, got, swap(add_low(keep[1::2], got[1::2]), 2)


def ring_rows(count, size):
    if count == 1:
        return [pl.ds(0, size)]
    me = lax.axis_index("dp")
    half = me >> 1
    place = jnp.where(me & 1 == 0, half, 7 - half)
    rows = []
    for k in range(count):
        at = (place + k) & 7
        owner = jnp.where(at < 4, 2 * at, 15 - 2 * at)
        rows.append(pl.ds(pl.multiple_of(owner * size, size), size))
    return rows


def pack_kernel(query, key, value, output, out):
    out[...] = jnp.concatenate(
        [query[...], key[...], value[...], jnp.transpose(output[...].astype(F32)).astype(BF)], axis=1
    )


def pack_experts_kernel(groups, w_in, w_out, *packed):
    for chosen, part in zip(groups, packed):
        for i, e in enumerate(chosen):
            part[i] = w_in[e]
            part[len(chosen) + i] = w_out[e]


def finish_kernel(groups, *refs):
    terms, (d_in, d_out) = refs[:-2], refs[-2:]
    for g, chosen in enumerate(groups):
        own, up, down = terms[3 * g : 3 * g + 3]
        for i in range(2 * len(chosen)):
            total = own[i].astype(F32) + up[i].astype(F32) + down[i].astype(F32)
            if i < len(chosen):
                d_in[chosen[i]] = total
            else:
                d_out[chosen[i - len(chosen)]] = total


def prepare_kernel(heads, experts, capacity, ids, pieces, buckets, table, rows, cols, wheel):
    seq = ids.shape[1]
    part = seq // 4
    me = lax.axis_index("tensor")
    seen = jnp.concatenate(
        [ids[:, pl.ds(pl.multiple_of((me ^ k) * part, part), part)] for k in range(4)], axis=1
    )
    chosen = lax.broadcasted_iota(jnp.int32, (8, seq), 0) == seen
    chosen = chosen.astype(F32)
    shape = (seq, seq)
    earlier = lax.broadcasted_iota(jnp.int32, shape, 0) < lax.broadcasted_iota(jnp.int32, shape, 1)
    rank = mm(chosen.astype(BF), earlier.astype(F32).astype(BF), NN)
    pos = jnp.sum(rank * chosen, axis=0, keepdims=True) + (seen * capacity).astype(F32)
    piece = pieces[...].astype(F32)
    held = jnp.concatenate(
        [pos, seen.astype(F32), jnp.where(piece > 0, piece, -1.0), jnp.zeros((5, seq), F32)], axis=0
    )
    rows[...] = held
    cols[...] = jnp.transpose(held)
    bucket = pltpu.roll(buckets[...], 2 * seq - (part - 1), 1)
    spread = lax.broadcasted_iota(jnp.int32, (table.shape[1], 2 * seq), 0) == bucket
    local = [table[pl.ds(me * heads + h, 1), :] for h in range(heads)]
    local.append(jnp.zeros((8 - heads, table.shape[1]), F32))
    wheel[...] = mm(jnp.concatenate(local, axis=0), spread.astype(F32), NN, HIGHEST)


def attention_forward_kernel(chunk_count, heads, *refs):
    x_refs, (gain, wheel, info_rows, info_cols) = refs[:4], refs[4:8]
    chunks = refs[8 : 8 + chunk_count]
    keep, send, qkv, ctx, lse, weight, bias, part, log_total = refs[8 + chunk_count :]
    rows = x_refs[0].shape[0]
    blocks = 4
    seq = rows * blocks
    me = lax.axis_index("tensor")
    width = heads * HEAD_DIM
    pad = 256
    for chunk, at in zip(chunks, ring_rows(chunk_count, chunks[0].shape[0])):
        size = chunk.shape[0]
        fill = jnp.zeros((size, pad - width), BF)
        whole = chunk[...]
        for s in range(4):
            weight[at, s * pad : (s + 1) * pad] = jnp.concatenate(
                [whole[:, s * width : (s + 1) * width], fill], axis=1
            )
    for k, x_ref in enumerate(x_refs):
        at = pl.ds(pl.multiple_of((me ^ k) * rows, rows), rows)
        wide = x_ref[...].astype(F32)
        low = (wide * rms_inverse(wide) * gain[...]).astype(BF)
        out = mm(low, weight[:, : 3 * pad], NN)
        qkv[at, :pad] = (out[:, :pad].astype(BF).astype(F32) * HEAD_DIM**-0.5).astype(BF)
        qkv[at, pad:] = out[:, pad:].astype(BF)
    lane = lax.broadcasted_iota(jnp.int32, (rows, 128), 1)
    ctx[...] = jnp.zeros_like(ctx)
    log_total[...] = jnp.zeros_like(log_total)

    def head_step(head, carry):
        pair = pl.multiple_of((head // 2) * 128, 128)
        mine = lane // HEAD_DIM == head % 2
        bias[...] = pltpu.roll(
            jnp.broadcast_to(wheel[pl.ds(head, 1), :], (rows, 2 * seq)), 0, 1, stride=1, stride_axis=0
        )
        for b in range(blocks):
            at = slice(b * rows, (b + 1) * rows)
            keys = min(b + 2, blocks) * rows
            q = jnp.where(mine, qkv[at, pl.ds(pair, 128)], jnp.zeros((), BF))
            k = qkv[:keys, pl.ds(pad + pair, 128)]
            v = qkv[:keys, pl.ds(2 * pad + pair, 128)]
            start = (blocks - 1 - b) * rows
            scores = mm(q, k, NT) + bias[:, start : start + keys]
            pieces = []
            if b:
                pieces.append(scores[:, : b * rows])
            tail = scores[:, b * rows :]
            shape = tail.shape
            piece = info_cols[at, 2:3]
            kept = (piece == info_rows[2:3, b * rows : keys]) & (piece > 0)
            kept = kept | (
                lax.broadcasted_iota(jnp.int32, shape, 1)
                <= lax.broadcasted_iota(jnp.int32, shape, 0)
            )
            pieces.append(jnp.where(kept, tail, NEG_LARGE))
            scores = jnp.concatenate(pieces, axis=1) if b else pieces[0]
            peak = jnp.max(scores, axis=-1, keepdims=True)
            prob = jnp.exp(scores - peak)
            total = jnp.sum(prob, axis=-1, keepdims=True)
            out = mm(prob.astype(BF), v, NN) / total
            ctx[at, pl.ds(pair, 128)] = jnp.where(mine, out.astype(BF), ctx[at, pl.ds(pair, 128)])
            log_total[at, :] = jnp.where(lane == head, peak + jnp.log(total), log_total[at, :])
        return carry

    lax.fori_loop(0, heads, head_step, 0)
    lse[...] = jnp.transpose(log_total[...])[:8]
    for b in range(blocks):
        part[me ^ b] = mm(ctx[b * rows : (b + 1) * rows, :], weight[:, 3 * pad :], NT).astype(BF)
    for k in range(2):
        keep[k] = part[2 * k]
        send[k] = part[2 * k + 1]


def attention_backward_kernel(owner_count, heads, pair_index, *refs):
    last = pair_index == 1
    d_refs, (wheel, buckets, info_rows, info_cols, qkv, ctx, lse, weight) = refs[:4], refs[4:12]
    refs = refs[12:]
    if last:
        x_refs, (gain, before, bias_before, d_qkv, bias_grad), refs = refs[:4], refs[4:9], refs[9:]
        outs, refs = refs[:owner_count], refs[owner_count:]
        grad, d_resid, normed, refs = *refs[:3], refs[3:]
    else:
        d_part, bias_grad, refs = refs[0], refs[1], refs[2:]
    d_ctx, d_q, d_k, d_v, slope, bias, d_bias = refs
    rows = d_refs[0].shape[0]
    blocks = 4
    seq = rows * blocks
    me = lax.axis_index("tensor")
    width = heads * HEAD_DIM
    pad = 256
    tiles = 2 * blocks - 1
    pair = 128 * pair_index
    here = slice(pair, pair + 128)
    for k, d_ref in enumerate(d_refs):
        at = pl.ds(pl.multiple_of((me ^ k) * rows, rows), rows)
        low = d_ref[...]
        if last:
            d_resid[at, :] = low
            wide = x_refs[k][...].astype(F32)
            normed[at, :] = (wide * rms_inverse(wide) * gain[...]).astype(BF)
        d_ctx[at, :] = mm(low, weight[:, 3 * pad + pair : 3 * pad + pair + 128], NN).astype(BF)
    lane = lax.broadcasted_iota(jnp.int32, (rows, 128), 1)
    d_q[...] = jnp.zeros_like(d_q)
    d_k[...] = jnp.zeros_like(d_k)
    d_v[...] = jnp.zeros_like(d_v)
    bias_grad[...] = bias_before[...] if last else jnp.zeros_like(bias_grad)
    none = jnp.zeros((), BF)
    bucket = pltpu.roll(buckets[...], 2 * seq - (rows - 1), 1)
    spread = lax.broadcasted_iota(jnp.int32, (bias_grad.shape[0], 2 * seq), 0) == bucket
    head_lane = lax.broadcasted_iota(jnp.int32, bias_grad.shape, 1)

    def head_step(head, carry):
        mine = lane // HEAD_DIM == head % 2
        slope[...] = pltpu.roll(
            jnp.broadcast_to(wheel[pl.ds(head, 1), :], (rows, 2 * seq)), 0, 1, stride=1, stride_axis=0
        )
        for a in range(tiles):
            bias[a] = jnp.transpose(slope[:, a * rows : (a + 1) * rows])
        d_bias[...] = jnp.zeros_like(d_bias)
        for b in range(blocks):
            at = slice(b * rows, (b + 1) * rows)
            q = jnp.where(mine, qkv[at, here], none)
            g = jnp.where(mine, d_ctx[at, :], none)
            base = jnp.sum(
                jnp.transpose(g.astype(F32) * ctx[at, here].astype(F32)), axis=0, keepdims=True
            )
            log_total = lse[pl.ds(head, 1), at]
            d_q_block = jnp.zeros((rows, 128), F32)
            for t in range(min(b + 2, blocks)):
                over = slice(t * rows, (t + 1) * rows)
                a = t - b + blocks - 1
                k = qkv[over, pad + pair : pad + pair + 128]
                scores = mm(k, q, NT) + bias[a]
                prob = jnp.exp(scores - log_total)
                if t >= b:
                    piece = info_cols[over, 2:3]
                    kept = (piece == info_rows[2:3, at]) & (piece > 0)
                    if t == b:
                        shape = (rows, rows)
                        kept = kept | (
                            lax.broadcasted_iota(jnp.int32, shape, 0)
                            <= lax.broadcasted_iota(jnp.int32, shape, 1)
                        )
                    prob = jnp.where(kept, prob, 0.0)
                d_v[over, :] += mm(prob.astype(BF), g, NN)
                d_prob = mm(qkv[over, 2 * pad + pair : 2 * pad + pair + 128], g, NT)
                d_score = (prob * (d_prob - base)).astype(BF)
                d_bias[a] += d_score.astype(F32)
                d_k[over, :] += mm(d_score, q, NN)
                d_q_block += mm(d_score, k, TN)
            d_q[at, :] += jnp.where(mine, d_q_block, 0.0)
        for a in range(tiles):
            slope[:, a * rows : (a + 1) * rows] = jnp.transpose(d_bias[a])
        slope[:, tiles * rows :] = jnp.zeros((rows, rows), F32)
        total = jnp.zeros((8, 2 * seq), F32)
        for g8 in range(rows // 8):
            total += pltpu.roll(slope[g8 * 8 : g8 * 8 + 8, :], (2 * seq - g8 * 8) % (2 * seq), 1)
        line = total[0:1]
        for s in range(1, 8):
            line += pltpu.roll(total, 2 * seq - s, 1)[s : s + 1]
        column = jnp.sum(jnp.where(spread, line, 0.0), axis=1, keepdims=True)
        bias_grad[...] = jnp.where(head_lane == me * heads + head, column, bias_grad[...])
        return carry

    lax.fori_loop(2 * pair_index, min(heads, 2 * pair_index + 2), head_step, 0)
    for s, value in enumerate((d_q[...] * HEAD_DIM**-0.5, d_k[...], d_v[...])):
        if last:
            d_qkv[:, s * pad : s * pad + pair] = before[:, s * 128 : (s + 1) * 128]
            d_qkv[:, s * pad + pair : (s + 1) * pad] = value.astype(BF)
        else:
            d_part[:, s * 128 : (s + 1) * 128] = value.astype(BF)
    if not last:
        return
    for s in range(3):
        out = mm(normed[...], d_qkv[:, s * pad : (s + 1) * pad], TN)
        grad[:, s * width : (s + 1) * width] = out[:, :width]
    grad[:, 3 * width :] = mm(d_resid[...], ctx[...], TN)[:, :width]
    span = grad.shape[0] // owner_count
    for out, at in zip(outs, ring_rows(owner_count, span)):
        out[:span, :] = grad[at, :].astype(BF)
        if out.shape[0] > span:
            out[span:, :] = jnp.zeros((out.shape[0] - span, out.shape[1]), BF)


def input_share_kernel(experts, *refs):
    x_refs = refs[:4]
    gain, d_qkv, weight, small, moe_gain_grad, bias_grad, keep, send, sums = refs[4:]
    rows, width = x_refs[0].shape
    me = lax.axis_index("tensor")
    total = jnp.zeros((1, width), F32)
    for k, x_ref in enumerate(x_refs):
        at = pl.ds(pl.multiple_of((me ^ k) * rows, rows), rows)
        wide = x_ref[...].astype(F32)
        inverse = rms_inverse(wide)
        unit = wide * inverse
        d_normed = mm(d_qkv[at, :], weight[:, :768], NT)
        total += jnp.sum(d_normed * unit, axis=0, keepdims=True)
        share = pullback(d_normed, unit, inverse, gain[...]).astype(BF)
        (send if k % 2 else keep)[k // 2] = share
    lines = [total, moe_gain_grad[...] + small[8:9, :]] + [small[e : e + 1, :] for e in range(experts)]
    sums[...] = jnp.zeros_like(sums)
    for i, line in enumerate(lines):
        sums[i : i + 1, :] = line
    for i in range(bias_grad.shape[0] // 8):
        sums[8:16, i * 128 : (i + 1) * 128] = bias_grad[i * 8 : i * 8 + 8, :]


def gelu_pair(u):
    c = float(np.sqrt(2.0 / np.pi))
    square = u * u
    t = jnp.tanh(c * u * (1.0 + 0.044715 * square))
    half = 0.5 * (1.0 + t)
    slope = half + 0.5 * c * u * (1.0 - t * t) * (1.0 + 3 * 0.044715 * square)
    return u * half, slope


def route(low, router, expert_col, experts):
    logits = mm(low, router, NN)
    lane = lax.broadcasted_iota(jnp.int32, logits.shape, 1)
    logits = jnp.where(lane < experts, logits, NEG_LARGE)
    grown = jnp.exp(logits - jnp.max(logits, axis=-1, keepdims=True))
    probs = grown / jnp.sum(grown, axis=-1, keepdims=True)
    onehot = (lane == expert_col).astype(F32)
    return probs, onehot, jnp.sum(probs * onehot, axis=-1, keepdims=True)


def moe_kernel(chunk_count, chosen, first, last, experts, capacity, *refs):
    kinds = len(chosen)
    r_refs, refs = refs[:4], refs[4:]
    gain, info_rows, info_cols, refs = refs[0], refs[1], refs[2], refs[3:]
    if first:
        g_refs, router, refs = refs[:4], refs[4], refs[5:]
    else:
        normed, d_token, before, refs = refs[0], refs[1], refs[2:4], refs[4:]
    chunks, refs = refs[:chunk_count], refs[chunk_count:]
    if first:
        normed, d_token, refs = refs[0], refs[1], refs[2:]
    if last:
        keep, send, gain_grad, refs = *refs[:3], refs[3:]
    else:
        out_part, grad_part, refs = refs[0], refs[1], refs[2:]
    outs, refs = refs[:chunk_count], refs[chunk_count:]
    weight, grad, out_slots, grad_slots = refs
    rows, width = r_refs[0].shape
    seq = 4 * rows
    tile = capacity // 2
    if first:
        for k in range(4):
            at = slice(k * rows, (k + 1) * rows)
            wide = r_refs[k][...].astype(F32)
            low = (wide * rms_inverse(wide) * gain[...]).astype(BF)
            normed[at, :] = low
            gate = route(low, router[...], info_cols[at, 1:2], experts)[2]
            d_token[at, :] = (gate * g_refs[k][...].astype(F32)).astype(BF)
    places = ring_rows(chunk_count, chunks[0].shape[1])
    slot = lax.broadcasted_iota(jnp.int32, (tile, seq), 0).astype(F32)
    for i, e in enumerate(chosen):
        held = jnp.sum((info_rows[1:2, :] == e).astype(F32))
        for chunk, place in zip(chunks, places):
            weight[0, place, :] = chunk[i]
            weight[1, place, :] = chunk[kinds + i]
        for t in range(2):
            base = (e * 2 + t) * tile
            at = slice((2 * i + t) * tile, (2 * i + t + 1) * tile)
            used = held > t * tile

            @pl.when(used)
            def _():
                pick = (info_rows[0:1, :] == slot + base).astype(F32).astype(BF)
                x = mm(pick, normed[...], NN).astype(BF)
                g = mm(pick, d_token[...], NN).astype(BF)
                hidden, slope = gelu_pair(mm(x, weight[0], NN))
                low = hidden.astype(BF)
                out_slots[at, :] = mm(low, weight[1], NT).astype(BF)
                d_pre = (mm(g, weight[1], NN) * slope).astype(BF)
                grad_slots[at, :] = mm(d_pre, weight[0], NT).astype(BF)
                d_in, d_out = mm(x, d_pre, TN), mm(g, low, TN)
                if t:
                    grad[0] += d_in
                    grad[1] += d_out
                else:
                    grad[0] = d_in
                    grad[1] = d_out

            @pl.when(jnp.logical_not(used))
            def _():
                out_slots[at, :] = jnp.zeros((tile, width), BF)
                grad_slots[at, :] = jnp.zeros((tile, width), BF)
                if not t:
                    grad[...] = jnp.zeros_like(grad)

        for out, place in zip(outs, places):
            out[i] = grad[0, place, :].astype(BF)
            out[kinds + i] = grad[1, place, :].astype(BF)
    if last:
        total = jnp.zeros(gain_grad.shape, F32)
    column = lax.broadcasted_iota(jnp.int32, (rows, 2 * kinds * tile), 1) + chosen[0] * 2 * tile
    column = column.astype(F32)
    for k in range(4):
        at = slice(k * rows, (k + 1) * rows)
        pick = (info_cols[at, 0:1] == column).astype(F32).astype(BF)
        out = mm(pick, out_slots[...], NN)
        d_normed = mm(pick, grad_slots[...], NN)
        if not first:
            out += before[0][k].astype(F32)
            d_normed += before[1][k].astype(F32)
        if last:
            (send if k % 2 else keep)[k // 2] = out.astype(BF)
            wide = r_refs[k][...].astype(F32)
            inverse = rms_inverse(wide)
            unit = wide * inverse
            total += jnp.sum(d_normed * unit, axis=0, keepdims=True)
            (send if k % 2 else keep)[2 + k // 2] = pullback(
                d_normed, unit, inverse, gain[...]
            ).astype(BF)
        else:
            out_part[k] = out.astype(BF)
            grad_part[k] = d_normed.astype(BF)
    if last:
        gain_grad[...] = total


def moe_call(operands, chunks, chosen, first, last, shape, experts, capacity):
    rows, width, hidden = shape
    kinds, count = 2 * len(chosen), len(chunks)
    outs = []
    if first:
        outs += [shaped((4 * rows, width), BF)] * 2
    if last:
        outs += [shaped((4, rows, width), BF)] * 2 + [shaped((1, width), F32)]
    else:
        outs += [shaped((4, rows, width), BF)] * 2
    scratch = [
        pltpu.VMEM((2, width, hidden), BF),
        pltpu.VMEM((2, width, hidden), F32),
        pltpu.VMEM((len(chosen) * capacity, width), BF),
        pltpu.VMEM((len(chosen) * capacity, width), BF),
    ]
    return call(
        "moe_last" if last else "moe",
        functools.partial(moe_kernel, count, chosen, first, last, experts, capacity),
        outs + [shaped((kinds, width // count, hidden), BF)] * count,
        [*operands, *chunks],
        scratch,
        6e9 * len(chosen),
    )


def join_kernel(
    experts, x, a0, a1, a2, m0, m1, m2, cotangent, gain, router, info_cols,
    output, d_resid, d_resid_low, small,
):
    def three(keep, got, across, n):
        return keep[2 * n].astype(F32) + got[2 * n].astype(F32) + across[n].astype(F32)

    rows = x.shape[0]
    residual = x[...].astype(F32) + three(a0, a1, a2, 0)
    expert_own = three(m0, m1, m2, 0)
    wide = residual.astype(BF).astype(F32)
    inverse = rms_inverse(wide)
    unit = wide * inverse
    low = (unit * gain[...]).astype(BF)
    probs, onehot, gate = route(low, router[...], info_cols[:rows, 1:2], experts)
    output[...] = (residual + gate * expert_own).astype(BF)
    cot = cotangent[...].astype(F32)
    d_gate = jnp.sum(cot * expert_own, axis=-1, keepdims=True)
    d_logits = d_gate * gate * (onehot - probs)
    d_rows = mm(d_logits, router[...].astype(F32), NT, HIGHEST)
    total = cot + three(m0, m1, m2, 1) + pullback(d_rows, unit, inverse, gain[...])
    d_resid[...] = total
    d_resid_low[...] = total.astype(BF)
    small[0:8, :] = mm(d_logits, low.astype(F32), TN, HIGHEST)[:8]
    small[8:9, :] = jnp.sum(d_rows * unit, axis=0, keepdims=True)
    small[9:16, :] = jnp.zeros_like(small[9:16, :])


def call(name, kernel, outs, operands, scratch=(), flops=1e8, specs=None, out_specs=None):
    moved = sum(v.size * v.dtype.itemsize for v in operands)
    moved += sum(int(np.prod(s.shape)) * s.dtype.itemsize for s in outs)
    return pl.pallas_call(
        kernel,
        name=name,
        out_shape=outs,
        in_specs=specs or [VMEM] * len(operands),
        out_specs=out_specs or [VMEM] * len(outs),
        scratch_shapes=scratch,
        compiler_params=pltpu.CompilerParams(vmem_limit_bytes=VMEM_MIB.get(name, 60) * 2**20),
        cost_estimate=pl.CostEstimate(flops=int(flops), bytes_accessed=moved, transcendentals=0),
    )(*operands)


def shaped(shape, dtype):
    return jax.ShapeDtypeStruct(shape, dtype)


def body(
    layer_input, out_grad, attention_norm_scale, expert_norm_scale, query_weight, key_weight,
    value_weight, output_weight, bias_table, router_weight, expert_in, expert_out, expert_ids,
    slot_ids, piece_ids, bucket_table,
):
    rows, width = layer_input.shape
    size = lax.axis_size("dp")
    seq = rows * 4
    heads = query_weight.shape[1] // HEAD_DIM
    experts = expert_in.shape[0]
    hidden = expert_in.shape[2]
    capacity = 2 * seq // experts
    head_count, bucket_count = bias_table.shape
    ring = use_ring(size)
    local = heads * HEAD_DIM
    span = query_weight.shape[0]
    count = size if ring else 1
    held = width // count
    groups = GROUPS

    (qkvo,) = call(
        "pack",
        pack_kernel,
        [shaped((span, 4 * local), BF)],
        [query_weight, key_weight, value_weight, output_weight],
    )
    packed = call(
        "pack_experts",
        functools.partial(pack_experts_kernel, groups),
        [shaped((2 * len(chosen), span, hidden), BF) for chosen in groups],
        [expert_in, jnp.transpose(expert_out, (0, 2, 1))],
    )
    buckets = jnp.pad(bucket_table, (0, 1), constant_values=-1).reshape(1, 2 * seq)
    info_rows, info_cols, wheel = call(
        "prepare",
        functools.partial(prepare_kernel, heads, experts, capacity),
        [shaped((8, seq), F32), shaped((seq, 8), F32), shaped((8, 2 * seq), F32)],
        [expert_ids.reshape(1, seq), piece_ids.reshape(1, seq), buckets, bias_table],
    )
    x_pieces = tensor_gather(layer_input, "gather_input", late=False)
    if ring:
        qkvo_chunks = ring_gather(
            qkvo, size, size // 2, "gather_qkvo", ((), tuple(packed), (info_rows, info_cols, wheel))
        )
        packed = [tie(v, qkvo_chunks[2], qkvo_chunks[6]) for v in packed]
        group_chunks = [
            ring_gather(v, size, size // 2 - 1 + g % 2, f"gather_experts{g}")
            for g, v in enumerate(packed)
        ]
    else:
        qkvo_chunks = [lax.all_gather(qkvo, "dp", axis=0, tiled=True)]
        group_chunks = [[lax.all_gather(v, "dp", axis=1, tiled=True)] for v in packed]
    g_pieces = tensor_gather(out_grad, "gather_cotangent")
    attn_gain = attention_norm_scale[None, :]
    moe_gain = expert_norm_scale[None, :]
    router = jnp.pad(router_weight, ((0, 0), (0, 128 - experts)))

    keep, send, qkv, ctx, lse, weight = call(
        "attention_forward", functools.partial(attention_forward_kernel, count, heads),
        [
            shaped((2, rows, width), BF), shaped((2, rows, width), BF), shaped((seq, 768), BF),
            shaped((seq, 256), BF), shaped((8, seq), F32), shaped((width, 1024), BF),
        ],
        [*x_pieces, attn_gain, wheel, info_rows, info_cols, *qkvo_chunks],
        [
            pltpu.VMEM((rows, 2 * seq), F32),
            pltpu.VMEM((4, rows, width), BF),
            pltpu.VMEM((seq, 128), F32),
        ],
        12e9,
    )
    if ring:
        send = tie(send, *(c[k] for c in group_chunks for k in (1, 7)), g_pieces[2])
    wait = (group_chunks[1][1], group_chunks[1][7]) if ring else ()
    a_parts = tensor_scatter(keep, send, "sum_attention")
    a_parts = (*a_parts[:2], tie(a_parts[2], *wait))
    resid_low = (
        layer_input.astype(F32)
        + (a_parts[0][0].astype(F32) + a_parts[1][0].astype(F32) + a_parts[2][0].astype(F32))
    ).astype(BF)
    if ring:
        resid_low = tie(resid_low, group_chunks[0][2], group_chunks[0][6])
    r_pieces = tensor_gather(resid_low, "gather_residual")

    expert_grads, group_grads, rings = [], [], []
    for g, chosen in enumerate(groups):
        first, last = g == 0, g == len(groups) - 1
        operands = [*r_pieces, moe_gain, info_rows, info_cols]
        if first:
            operands += [*g_pieces, router]
        else:
            operands += [normed_two, d_token, out_part, grad_part]
        results = moe_call(
            operands, group_chunks[g], chosen, first, last, (rows, width, hidden), experts, capacity
        )
        if first:
            normed_two, d_token, results = results[0], results[1], results[2:]
        if last:
            keep, send, moe_gain_grad, results = *results[:3], results[3:]
        else:
            out_part, grad_part, results = results[0], results[1], results[2:]
        if ring:
            hops = ring_scatter(results, size, size // 2 - 1 + g % 2, f"sum_grads{g}")
            next(hops)
            rings.append(hops)
            if first:
                early = hops.send(())
        else:
            total = lax.psum_scatter(results[0].astype(F32), "dp", scatter_dimension=1, tiled=True)
            expert_grads.append(total)
        group_grads.append(results)
    if ring:
        send = tie(send, *early)
    m_parts = tensor_scatter(keep, send, "sum_experts_d_resid")
    if ring:
        wait = (m_parts[1],)
        arrived = [hops.send(wait) for hops in rings]

    layer_output, d_resid, d_resid_low, small = call(
        "join", functools.partial(join_kernel, experts),
        [
            shaped((rows, width), BF), shaped((rows, width), F32), shaped((rows, width), BF),
            shaped((16, width), F32),
        ],
        [
            layer_input, *a_parts, *m_parts,
            out_grad, moe_gain, router, info_cols,
        ],
        flops=1e9,
    )
    if ring:
        arrived[0] = rings[0].send(())
    d_pieces = tensor_gather(d_resid_low, "gather_d_resid")
    if ring:
        wheel = tie(wheel, *arrived[1])
        arrived[1] = rings[1].send(())

    tiles = 7
    shared = [
        pltpu.VMEM((seq, 128), BF),
        pltpu.VMEM((seq, 128), F32),
        pltpu.VMEM((seq, 128), F32),
        pltpu.VMEM((seq, 128), F32),
        pltpu.VMEM((rows, 2 * seq), F32),
        pltpu.VMEM((tiles, rows, rows), F32),
        pltpu.VMEM((tiles, rows, rows), F32),
    ]
    operands = [*d_pieces, wheel, buckets, info_rows, info_cols, qkv, ctx, lse, weight]
    d_part, bias_grad = call(
        "attention_backward0",
        functools.partial(attention_backward_kernel, count, heads, 0),
        [shaped((seq, 384), BF), shaped((bucket_count, 128), F32)],
        operands,
        shared,
        12e9,
    )
    if ring:
        wait = (d_part,)
        d_part = tie(d_part, *arrived[0])
        arrived[0] = rings[0].send(wait)
    d_qkv, bias_grad, *qkvo_grads = call(
        "attention_backward1",
        functools.partial(attention_backward_kernel, count, heads, 1),
        [
            shaped((seq, 768), BF), shaped((bucket_count, 128), F32),
            *[shaped((held + SMALL * ring, 4 * local), BF)] * count,
        ],
        [*operands, *x_pieces, attn_gain, d_part, bias_grad],
        [
            pltpu.VMEM((width, 4 * local), F32),
            pltpu.VMEM((seq, width), BF),
            pltpu.VMEM((seq, width), BF),
            *shared,
        ],
        12e9,
    )
    if ring:
        wait = (d_qkv,)
        d_qkv = tie(d_qkv, *arrived[1], *arrived[0])
        arrived[1] = rings[1].send(wait)
    keep, send, sums = call(
        "input_share", functools.partial(input_share_kernel, experts),
        [
            shaped((2, rows, width), BF), shaped((2, rows, width), BF), shaped((SMALL, width), F32),
        ],
        [*x_pieces, attn_gain, d_qkv, weight, small, moe_gain_grad, bias_grad],
        flops=2e9,
    )
    if ring:
        arrived[1] = rings[1].send(())
    i0, i1, i2 = tensor_scatter(keep, send, "sum_input_grad")
    input_grad = (
        d_resid + (i0[0].astype(F32) + i1[0].astype(F32) + i2[0].astype(F32))
    ).astype(BF)
    if ring:
        own = jnp.pad(sums.astype(BF), ((held, 0), (0, 0)))
        sent = [v + own if k in (3, 4) else v for k, v in enumerate(qkvo_grads)]
        hops = ring_scatter(sent, size, 3, "sum_grads_qkvo")
        next(hops)
        sums = own[held:].astype(F32)
        for hop in range(4):
            qkvo_up, qkvo_down = hops.send((i1,) if hop == 1 else ())
            if hop == 2:
                qkvo_late = qkvo_down
            sums = sums + qkvo_down[held:].astype(F32)
            if hop < 3:
                sums = sums + qkvo_up[held:].astype(F32)
    else:
        sums = lax.psum(sums, "dp")
    sums = sums + swap(sums, 1)
    sums = sums + swap(sums, 2)
    grad_attn_gain, grad_moe_gain = sums[0], sums[1]
    grad_router = jnp.transpose(sums[2 : 2 + experts])
    grad_bias_table = jnp.transpose(
        jnp.concatenate(
            [sums[8:16, i * 128 : i * 128 + head_count] for i in range(bucket_count // 8)], axis=0
        )
    )
    if ring:
        qkvo_grad = (
            qkvo_grads[0].astype(F32) + qkvo_up.astype(F32) + qkvo_down.astype(F32)
        )[:held]
        group_grads[0] = [tie(group_grads[0][0], qkvo_late)]
        grad_in, grad_out = call(
            "finish",
            functools.partial(finish_kernel, groups),
            [shaped((experts, span, hidden), F32)] * 2,
            [v for parts, came in zip(group_grads, arrived) for v in (parts[0], *came)],
        )
    else:
        qkvo_grad = lax.psum_scatter(
            qkvo_grads[0].astype(F32), "dp", scatter_dimension=0, tiled=True
        )
        kinds = [len(chosen) for chosen in groups]
        grad_in = jnp.concatenate([v[:n] for v, n in zip(expert_grads, kinds)], axis=0)
        grad_out = jnp.concatenate([v[n:] for v, n in zip(expert_grads, kinds)], axis=0)
    grad_query, grad_key, grad_value = (
        qkvo_grad[:, s * local : (s + 1) * local] for s in range(3)
    )
    grad_output = jnp.transpose(qkvo_grad[:, 3 * local :])
    grad_out = jnp.transpose(grad_out, (0, 2, 1))
    return (
        layer_output, input_grad, grad_attn_gain, grad_moe_gain, grad_query, grad_key, grad_value,
        grad_output, grad_bias_table, grad_router, grad_in, grad_out,
    )


def solution(mesh):
    in_specs = (
        P(("dp", "tensor"), None),
        P(("dp", "tensor"), None),
        P(),
        P(),
        P("dp", "tensor"),
        P("dp", "tensor"),
        P("dp", "tensor"),
        P("tensor", "dp"),
        P(),
        P(),
        P(None, "dp", "tensor"),
        P(None, "tensor", "dp"),
        P("dp"),
        P("dp"),
        P("dp"),
        P(),
    )
    out_specs = (
        P(("dp", "tensor"), None),
        P(("dp", "tensor"), None),
        P(),
        P(),
        P("dp", "tensor"),
        P("dp", "tensor"),
        P("dp", "tensor"),
        P("tensor", "dp"),
        P(),
        P(),
        P(None, "dp", "tensor"),
        P(None, "tensor", "dp"),
    )
    return jax.shard_map(body, mesh=mesh, in_specs=in_specs, out_specs=out_specs, check_vma=False)
```

```python
import functools

import jax
import jax.numpy as jnp
import numpy as np
from jax import lax
from jax.experimental import pallas as pl
from jax.experimental.pallas import tpu as pltpu
from jax.sharding import PartitionSpec as P

HEAD_DIM = 64
EPSILON = 1e-06
NEG_LARGE = -1e30
HIGHEST = lax.Precision.HIGHEST
BF = jnp.bfloat16
F32 = jnp.float32
NN = (((1,), (0,)), ((), ()))
NT = (((1,), (1,)), ((), ()))
TN = (((0,), (0,)), ((), ()))
VMEM = pl.BlockSpec(memory_space=pltpu.VMEM)
SMALL = 16
GROUPS = ((0, 1), (2, 3))
VMEM_MIB = {
    "pack": 4, "pack_experts": 8, "prepare": 12, "attention_forward": 28, "moe": 60, "moe_last": 60, "join": 14,
    "attention_backward0": 24, "attention_backward1": 28, "input_share": 16, "finish": 16,
}


def mm(left, right, dims, precision=None):
    return lax.dot_general(left, right, dims, preferred_element_type=F32, precision=precision)


def rms_inverse(rows):
    return lax.rsqrt(jnp.mean(rows * rows, axis=-1, keepdims=True) + EPSILON)


def pullback(grad, unit, inverse, gain):
    scaled = grad * gain
    return inverse * (scaled - unit * jnp.mean(scaled * unit, axis=-1, keepdims=True))


def tie(value, *others):
    if not others:
        return value
    return lax.optimization_barrier((value, *others))[0]


def ring_order(size):
    if size == 8:
        return (0, 2, 4, 6, 7, 5, 3, 1)
    return tuple(range(size))


def ring_perms(size):
    order = ring_order(size)
    ahead = [(order[i], order[(i + 1) % size]) for i in range(size)]
    return ahead, [(b, a) for a, b in ahead]


def use_ring(size):
    return size == 8


def ring_gather(chunk, size, far, name, waits=()):
    ahead, back = ring_perms(size)
    chunks = [chunk] + [None] * (size - 1)
    up = down = chunk
    for step in range(1, size):
        wait = waits[step - 1] if step <= len(waits) else ()
        if step <= far:
            with jax.named_scope(f"{name}_up{step}"):
                up = lax.ppermute(tie(up, *wait), "dp", ahead)
            chunks[size - step] = up
        if step <= size - 1 - far:
            with jax.named_scope(f"{name}_down{step}"):
                down = lax.ppermute(tie(down, *wait), "dp", back)
            chunks[step] = down
    return chunks


def add_low(left, right):
    return (left.astype(F32) + right.astype(F32)).astype(BF)


def ring_scatter(parts, size, far, name):
    ahead, back = ring_perms(size)
    near = size - 1 - far
    up, down = parts[far], parts[size - near]
    for step in range(max(far, near) + 1):
        wait = yield up, down
        if step < far:
            if step:
                up = add_low(up, parts[far - step])
            with jax.named_scope(f"{name}_up{step + 1}"):
                up = lax.ppermute(tie(up, *wait), "dp", ahead)
        if step < near:
            if step:
                down = add_low(down, parts[size - near + step])
            with jax.named_scope(f"{name}_down{step + 1}"):
                down = lax.ppermute(tie(down, *wait), "dp", back)


def tensor_perm(flip):
    return [(i, i ^ flip) for i in range(4)]


def swap(value, flip):
    return lax.ppermute(value, "tensor", tensor_perm(flip))


def tensor_gather(rows, name, late=True):
    with jax.named_scope(name):
        across = swap(rows, 2)
        beside = swap(rows, 1)
        return rows, beside, across, swap(across, 1)


def tensor_scatter(keep, send, name):
    with jax.named_scope(name):
        got = swap(send, 1)
        return keep, got, swap(add_low(keep[1::2], got[1::2]), 2)


def ring_rows(count, size):
    if count == 1:
        return [pl.ds(0, size)]
    me = lax.axis_index("dp")
    half = me >> 1
    place = jnp.where(me & 1 == 0, half, 7 - half)
    rows = []
    for k in range(count):
        at = (place + k) & 7
        owner = jnp.where(at < 4, 2 * at, 15 - 2 * at)
        rows.append(pl.ds(pl.multiple_of(owner * size, size), size))
    return rows


def pack_kernel(query, key, value, output, out):
    out[...] = jnp.concatenate(
        [query[...], key[...], value[...], jnp.transpose(output[...].astype(F32)).astype(BF)], axis=1
    )


def pack_experts_kernel(groups, w_in, w_out, *packed):
    for chosen, part in zip(groups, packed):
        for i, e in enumerate(chosen):
            part[i] = w_in[e]
            part[len(chosen) + i] = w_out[e]


def finish_kernel(groups, *refs):
    terms, (d_in, d_out) = refs[:-2], refs[-2:]
    for g, chosen in enumerate(groups):
        own, up, down = terms[3 * g : 3 * g + 3]
        for i in range(2 * len(chosen)):
            total = own[i].astype(F32) + up[i].astype(F32) + down[i].astype(F32)
            if i < len(chosen):
                d_in[chosen[i]] = total
            else:
                d_out[chosen[i - len(chosen)]] = total


def prepare_kernel(heads, experts, capacity, ids, pieces, buckets, table, rows, cols, wheel):
    seq = ids.shape[1]
    part = seq // 4
    me = lax.axis_index("tensor")
    seen = jnp.concatenate(
        [ids[:, pl.ds(pl.multiple_of((me ^ k) * part, part), part)] for k in range(4)], axis=1
    )
    chosen = lax.broadcasted_iota(jnp.int32, (8, seq), 0) == seen
    chosen = chosen.astype(F32)
    shape = (seq, seq)
    earlier = lax.broadcasted_iota(jnp.int32, shape, 0) < lax.broadcasted_iota(jnp.int32, shape, 1)
    rank = mm(chosen.astype(BF), earlier.astype(F32).astype(BF), NN)
    pos = jnp.sum(rank * chosen, axis=0, keepdims=True) + (seen * capacity).astype(F32)
    piece = pieces[...].astype(F32)
    held = jnp.concatenate(
        [pos, seen.astype(F32), jnp.where(piece > 0, piece, -1.0), jnp.zeros((5, seq), F32)], axis=0
    )
    rows[...] = held
    cols[...] = jnp.transpose(held)
    bucket = pltpu.roll(buckets[...], 2 * seq - (part - 1), 1)
    spread = lax.broadcasted_iota(jnp.int32, (table.shape[1], 2 * seq), 0) == bucket
    local = [table[pl.ds(me * heads + h, 1), :] for h in range(heads)]
    local.append(jnp.zeros((8 - heads, table.shape[1]), F32))
    wheel[...] = mm(jnp.concatenate(local, axis=0), spread.astype(F32), NN, HIGHEST)


def attention_forward_kernel(chunk_count, heads, *refs):
    x_refs, (gain, wheel, info_rows, info_cols) = refs[:4], refs[4:8]
    chunks = refs[8 : 8 + chunk_count]
    keep, send, qkv, ctx, lse, weight, bias, part, log_total = refs[8 + chunk_count :]
    rows = x_refs[0].shape[0]
    blocks = 4
    seq = rows * blocks
    me = lax.axis_index("tensor")
    width = heads * HEAD_DIM
    pad = 256
    for chunk, at in zip(chunks, ring_rows(chunk_count, chunks[0].shape[0])):
        size = chunk.shape[0]
        fill = jnp.zeros((size, pad - width), BF)
        whole = chunk[...]
        for s in range(4):
            weight[at, s * pad : (s + 1) * pad] = jnp.concatenate(
                [whole[:, s * width : (s + 1) * width], fill], axis=1
            )
    for k, x_ref in enumerate(x_refs):
        at = pl.ds(pl.multiple_of((me ^ k) * rows, rows), rows)
        wide = x_ref[...].astype(F32)
        low = (wide * rms_inverse(wide) * gain[...]).astype(BF)
        out = mm(low, weight[:, : 3 * pad], NN)
        qkv[at, :pad] = (out[:, :pad].astype(BF).astype(F32) * HEAD_DIM**-0.5).astype(BF)
        qkv[at, pad:] = out[:, pad:].astype(BF)
    lane = lax.broadcasted_iota(jnp.int32, (rows, 128), 1)
    ctx[...] = jnp.zeros_like(ctx)
    log_total[...] = jnp.zeros_like(log_total)

    def head_step(head, carry):
        pair = pl.multiple_of((head // 2) * 128, 128)
        mine = lane // HEAD_DIM == head % 2
        bias[...] = pltpu.roll(
            jnp.broadcast_to(wheel[pl.ds(head, 1), :], (rows, 2 * seq)), 0, 1, stride=1, stride_axis=0
        )
        for b in range(blocks):
            at = slice(b * rows, (b + 1) * rows)
            keys = min(b + 2, blocks) * rows
            q = jnp.where(mine, qkv[at, pl.ds(pair, 128)], jnp.zeros((), BF))
            k = qkv[:keys, pl.ds(pad + pair, 128)]
            v = qkv[:keys, pl.ds(2 * pad + pair, 128)]
            start = (blocks - 1 - b) * rows
            scores = mm(q, k, NT) + bias[:, start : start + keys]
            pieces = []
            if b:
                pieces.append(scores[:, : b * rows])
            tail = scores[:, b * rows :]
            shape = tail.shape
            piece = info_cols[at, 2:3]
            kept = (piece == info_rows[2:3, b * rows : keys]) & (piece > 0)
            kept = kept | (
                lax.broadcasted_iota(jnp.int32, shape, 1)
                <= lax.broadcasted_iota(jnp.int32, shape, 0)
            )
            pieces.append(jnp.where(kept, tail, NEG_LARGE))
            scores = jnp.concatenate(pieces, axis=1) if b else pieces[0]
            peak = jnp.max(scores, axis=-1, keepdims=True)
            prob = jnp.exp(scores - peak)
            total = jnp.sum(prob, axis=-1, keepdims=True)
            out = mm(prob.astype(BF), v, NN) / total
            ctx[at, pl.ds(pair, 128)] = jnp.where(mine, out.astype(BF), ctx[at, pl.ds(pair, 128)])
            log_total[at, :] = jnp.where(lane == head, peak + jnp.log(total), log_total[at, :])
        return carry

    lax.fori_loop(0, heads, head_step, 0)
    lse[...] = jnp.transpose(log_total[...])[:8]
    for b in range(blocks):
        part[me ^ b] = mm(ctx[b * rows : (b + 1) * rows, :], weight[:, 3 * pad :], NT).astype(BF)
    for k in range(2):
        keep[k] = part[2 * k]
        send[k] = part[2 * k + 1]


def attention_backward_kernel(owner_count, heads, pair_index, *refs):
    last = pair_index == 1
    d_refs, (wheel, buckets, info_rows, info_cols, qkv, ctx, lse, weight) = refs[:4], refs[4:12]
    refs = refs[12:]
    if last:
        x_refs, (gain, before, bias_before, d_qkv, bias_grad), refs = refs[:4], refs[4:9], refs[9:]
        outs, refs = refs[:owner_count], refs[owner_count:]
        grad, d_resid, normed, refs = *refs[:3], refs[3:]
    else:
        d_part, bias_grad, refs = refs[0], refs[1], refs[2:]
    d_ctx, d_q, d_k, d_v, slope, bias, d_bias = refs
    rows = d_refs[0].shape[0]
    blocks = 4
    seq = rows * blocks
    me = lax.axis_index("tensor")
    width = heads * HEAD_DIM
    pad = 256
    tiles = 2 * blocks - 1
    pair = 128 * pair_index
    here = slice(pair, pair + 128)
    for k, d_ref in enumerate(d_refs):
        at = pl.ds(pl.multiple_of((me ^ k) * rows, rows), rows)
        low = d_ref[...]
        if last:
            d_resid[at, :] = low
            wide = x_refs[k][...].astype(F32)
            normed[at, :] = (wide * rms_inverse(wide) * gain[...]).astype(BF)
        d_ctx[at, :] = mm(low, weight[:, 3 * pad + pair : 3 * pad + pair + 128], NN).astype(BF)
    lane = lax.broadcasted_iota(jnp.int32, (rows, 128), 1)
    d_q[...] = jnp.zeros_like(d_q)
    d_k[...] = jnp.zeros_like(d_k)
    d_v[...] = jnp.zeros_like(d_v)
    bias_grad[...] = bias_before[...] if last else jnp.zeros_like(bias_grad)
    none = jnp.zeros((), BF)
    bucket = pltpu.roll(buckets[...], 2 * seq - (rows - 1), 1)
    spread = lax.broadcasted_iota(jnp.int32, (bias_grad.shape[0], 2 * seq), 0) == bucket
    head_lane = lax.broadcasted_iota(jnp.int32, bias_grad.shape, 1)

    def head_step(head, carry):
        mine = lane // HEAD_DIM == head % 2
        slope[...] = pltpu.roll(
            jnp.broadcast_to(wheel[pl.ds(head, 1), :], (rows, 2 * seq)), 0, 1, stride=1, stride_axis=0
        )
        for a in range(tiles):
            bias[a] = jnp.transpose(slope[:, a * rows : (a + 1) * rows])
        d_bias[...] = jnp.zeros_like(d_bias)
        for b in range(blocks):
            at = slice(b * rows, (b + 1) * rows)
            q = jnp.where(mine, qkv[at, here], none)
            g = jnp.where(mine, d_ctx[at, :], none)
            base = jnp.sum(
                jnp.transpose(g.astype(F32) * ctx[at, here].astype(F32)), axis=0, keepdims=True
            )
            log_total = lse[pl.ds(head, 1), at]
            d_q_block = jnp.zeros((rows, 128), F32)
            for t in range(min(b + 2, blocks)):
                over = slice(t * rows, (t + 1) * rows)
                a = t - b + blocks - 1
                k = qkv[over, pad + pair : pad + pair + 128]
                scores = mm(k, q, NT) + bias[a]
                prob = jnp.exp(scores - log_total)
                if t >= b:
                    piece = info_cols[over, 2:3]
                    kept = (piece == info_rows[2:3, at]) & (piece > 0)
                    if t == b:
                        shape = (rows, rows)
                        kept = kept | (
                            lax.broadcasted_iota(jnp.int32, shape, 0)
                            <= lax.broadcasted_iota(jnp.int32, shape, 1)
                        )
                    prob = jnp.where(kept, prob, 0.0)
                d_v[over, :] += mm(prob.astype(BF), g, NN)
                d_prob = mm(qkv[over, 2 * pad + pair : 2 * pad + pair + 128], g, NT)
                d_score = (prob * (d_prob - base)).astype(BF)
                d_bias[a] += d_score.astype(F32)
                d_k[over, :] += mm(d_score, q, NN)
                d_q_block += mm(d_score, k, TN)
            d_q[at, :] += jnp.where(mine, d_q_block, 0.0)
        for a in range(tiles):
            slope[:, a * rows : (a + 1) * rows] = jnp.transpose(d_bias[a])
        slope[:, tiles * rows :] = jnp.zeros((rows, rows), F32)
        total = jnp.zeros((8, 2 * seq), F32)
        for g8 in range(rows // 8):
            total += pltpu.roll(slope[g8 * 8 : g8 * 8 + 8, :], (2 * seq - g8 * 8) % (2 * seq), 1)
        line = total[0:1]
        for s in range(1, 8):
            line += pltpu.roll(total, 2 * seq - s, 1)[s : s + 1]
        column = jnp.sum(jnp.where(spread, line, 0.0), axis=1, keepdims=True)
        bias_grad[...] = jnp.where(head_lane == me * heads + head, column, bias_grad[...])
        return carry

    lax.fori_loop(2 * pair_index, min(heads, 2 * pair_index + 2), head_step, 0)
    for s, value in enumerate((d_q[...] * HEAD_DIM**-0.5, d_k[...], d_v[...])):
        if last:
            d_qkv[:, s * pad : s * pad + pair] = before[:, s * 128 : (s + 1) * 128]
            d_qkv[:, s * pad + pair : (s + 1) * pad] = value.astype(BF)
        else:
            d_part[:, s * 128 : (s + 1) * 128] = value.astype(BF)
    if not last:
        return
    out = mm(normed[...], d_qkv[...], TN)
    for s in range(3):
        grad[:, s * width : (s + 1) * width] = out[:, s * pad : s * pad + width]
    grad[:, 3 * width :] = mm(d_resid[...], ctx[...], TN)[:, :width]
    span = grad.shape[0] // owner_count
    for out, at in zip(outs, ring_rows(owner_count, span)):
        out[:span, :] = grad[at, :].astype(BF)
        if out.shape[0] > span:
            out[span:, :] = jnp.zeros((out.shape[0] - span, out.shape[1]), BF)


def input_share_kernel(experts, *refs):
    x_refs = refs[:4]
    gain, d_qkv, weight, small, moe_gain_grad, bias_grad, keep, send, sums = refs[4:]
    rows, width = x_refs[0].shape
    me = lax.axis_index("tensor")
    total = jnp.zeros((1, width), F32)
    for k, x_ref in enumerate(x_refs):
        at = pl.ds(pl.multiple_of((me ^ k) * rows, rows), rows)
        wide = x_ref[...].astype(F32)
        inverse = rms_inverse(wide)
        unit = wide * inverse
        d_normed = mm(d_qkv[at, :], weight[:, :768], NT)
        total += jnp.sum(d_normed * unit, axis=0, keepdims=True)
        share = pullback(d_normed, unit, inverse, gain[...]).astype(BF)
        (send if k % 2 else keep)[k // 2] = share
    lines = [total, moe_gain_grad[...] + small[8:9, :]] + [small[e : e + 1, :] for e in range(experts)]
    sums[...] = jnp.zeros_like(sums)
    for i, line in enumerate(lines):
        sums[i : i + 1, :] = line
    for i in range(bias_grad.shape[0] // 8):
        sums[8:16, i * 128 : (i + 1) * 128] = bias_grad[i * 8 : i * 8 + 8, :]


def gelu_pair(u):
    c = float(np.sqrt(2.0 / np.pi))
    square = u * u
    t = jnp.tanh(c * u * (1.0 + 0.044715 * square))
    half = 0.5 * (1.0 + t)
    slope = half + 0.5 * c * u * (1.0 - t * t) * (1.0 + 3 * 0.044715 * square)
    return u * half, slope


def route(low, router, expert_col, experts):
    logits = mm(low, router, NN)
    lane = lax.broadcasted_iota(jnp.int32, logits.shape, 1)
    logits = jnp.where(lane < experts, logits, NEG_LARGE)
    grown = jnp.exp(logits - jnp.max(logits, axis=-1, keepdims=True))
    probs = grown / jnp.sum(grown, axis=-1, keepdims=True)
    onehot = (lane == expert_col).astype(F32)
    return probs, onehot, jnp.sum(probs * onehot, axis=-1, keepdims=True)


def moe_kernel(chunk_count, chosen, first, last, experts, capacity, *refs):
    kinds = len(chosen)
    r_refs, refs = refs[:4], refs[4:]
    gain, info_rows, info_cols, refs = refs[0], refs[1], refs[2], refs[3:]
    if first:
        g_refs, router, refs = refs[:4], refs[4], refs[5:]
    else:
        normed, d_token, before, refs = refs[0], refs[1], refs[2:4], refs[4:]
    chunks, refs = refs[:chunk_count], refs[chunk_count:]
    if first:
        normed, d_token, refs = refs[0], refs[1], refs[2:]
    if last:
        keep, send, gain_grad, refs = *refs[:3], refs[3:]
    else:
        out_part, grad_part, refs = refs[0], refs[1], refs[2:]
    outs, refs = refs[:chunk_count], refs[chunk_count:]
    weight, grad, out_slots, grad_slots = refs
    rows, width = r_refs[0].shape
    seq = 4 * rows
    tile = capacity // 2
    if first:
        for k in range(4):
            at = slice(k * rows, (k + 1) * rows)
            wide = r_refs[k][...].astype(F32)
            low = (wide * rms_inverse(wide) * gain[...]).astype(BF)
            normed[at, :] = low
            gate = route(low, router[...], info_cols[at, 1:2], experts)[2]
            d_token[at, :] = (gate * g_refs[k][...].astype(F32)).astype(BF)
    places = ring_rows(chunk_count, chunks[0].shape[1])
    slot = lax.broadcasted_iota(jnp.int32, (tile, seq), 0).astype(F32)
    for i, e in enumerate(chosen):
        held = jnp.sum((info_rows[1:2, :] == e).astype(F32))
        for chunk, place in zip(chunks, places):
            weight[0, place, :] = chunk[i]
            weight[1, place, :] = chunk[kinds + i]
        for t in range(2):
            base = (e * 2 + t) * tile
            at = slice((2 * i + t) * tile, (2 * i + t + 1) * tile)
            used = held > t * tile

            @pl.when(used)
            def _():
                pick = (info_rows[0:1, :] == slot + base).astype(F32).astype(BF)
                x = mm(pick, normed[...], NN).astype(BF)
                g = mm(pick, d_token[...], NN).astype(BF)
                hidden, slope = gelu_pair(mm(x, weight[0], NN))
                low = hidden.astype(BF)
                out_slots[at, :] = mm(low, weight[1], NT).astype(BF)
                d_pre = (mm(g, weight[1], NN) * slope).astype(BF)
                grad_slots[at, :] = mm(d_pre, weight[0], NT).astype(BF)
                d_in, d_out = mm(x, d_pre, TN), mm(g, low, TN)
                if t:
                    grad[0] += d_in
                    grad[1] += d_out
                else:
                    grad[0] = d_in
                    grad[1] = d_out

            @pl.when(jnp.logical_not(used))
            def _():
                out_slots[at, :] = jnp.zeros((tile, width), BF)
                grad_slots[at, :] = jnp.zeros((tile, width), BF)
                if not t:
                    grad[...] = jnp.zeros_like(grad)

        for out, place in zip(outs, places):
            out[i] = grad[0, place, :].astype(BF)
            out[kinds + i] = grad[1, place, :].astype(BF)
    if last:
        total = jnp.zeros(gain_grad.shape, F32)
    column = lax.broadcasted_iota(jnp.int32, (rows, 2 * kinds * tile), 1) + chosen[0] * 2 * tile
    column = column.astype(F32)
    for k in range(4):
        at = slice(k * rows, (k + 1) * rows)
        pick = (info_cols[at, 0:1] == column).astype(F32).astype(BF)
        out = mm(pick, out_slots[...], NN)
        d_normed = mm(pick, grad_slots[...], NN)
        if not first:
            out += before[0][k].astype(F32)
            d_normed += before[1][k].astype(F32)
        if last:
            (send if k % 2 else keep)[k // 2] = out.astype(BF)
            wide = r_refs[k][...].astype(F32)
            inverse = rms_inverse(wide)
            unit = wide * inverse
            total += jnp.sum(d_normed * unit, axis=0, keepdims=True)
            (send if k % 2 else keep)[2 + k // 2] = pullback(
                d_normed, unit, inverse, gain[...]
            ).astype(BF)
        else:
            out_part[k] = out.astype(BF)
            grad_part[k] = d_normed.astype(BF)
    if last:
        gain_grad[...] = total


def moe_call(operands, chunks, chosen, first, last, shape, experts, capacity):
    rows, width, hidden = shape
    kinds, count = 2 * len(chosen), len(chunks)
    outs = []
    if first:
        outs += [shaped((4 * rows, width), BF)] * 2
    if last:
        outs += [shaped((4, rows, width), BF)] * 2 + [shaped((1, width), F32)]
    else:
        outs += [shaped((4, rows, width), BF)] * 2
    scratch = [
        pltpu.VMEM((2, width, hidden), BF),
        pltpu.VMEM((2, width, hidden), F32),
        pltpu.VMEM((len(chosen) * capacity, width), BF),
        pltpu.VMEM((len(chosen) * capacity, width), BF),
    ]
    return call(
        "moe_last" if last else "moe",
        functools.partial(moe_kernel, count, chosen, first, last, experts, capacity),
        outs + [shaped((kinds, width // count, hidden), BF)] * count,
        [*operands, *chunks],
        scratch,
        6e9 * len(chosen),
    )


def join_kernel(
    experts, x, a0, a1, a2, m0, m1, m2, cotangent, gain, router, info_cols,
    output, d_resid, d_resid_low, small,
):
    def three(keep, got, across, n):
        return keep[2 * n].astype(F32) + got[2 * n].astype(F32) + across[n].astype(F32)

    rows = x.shape[0]
    residual = x[...].astype(F32) + three(a0, a1, a2, 0)
    expert_own = three(m0, m1, m2, 0)
    wide = residual.astype(BF).astype(F32)
    inverse = rms_inverse(wide)
    unit = wide * inverse
    low = (unit * gain[...]).astype(BF)
    probs, onehot, gate = route(low, router[...], info_cols[:rows, 1:2], experts)
    output[...] = (residual + gate * expert_own).astype(BF)
    cot = cotangent[...].astype(F32)
    d_gate = jnp.sum(cot * expert_own, axis=-1, keepdims=True)
    d_logits = d_gate * gate * (onehot - probs)
    d_rows = mm(d_logits, router[...].astype(F32), NT, HIGHEST)
    total = cot + three(m0, m1, m2, 1) + pullback(d_rows, unit, inverse, gain[...])
    d_resid[...] = total
    d_resid_low[...] = total.astype(BF)
    small[0:8, :] = mm(d_logits, low.astype(F32), TN, HIGHEST)[:8]
    small[8:9, :] = jnp.sum(d_rows * unit, axis=0, keepdims=True)
    small[9:16, :] = jnp.zeros_like(small[9:16, :])


def call(name, kernel, outs, operands, scratch=(), flops=1e8, specs=None, out_specs=None):
    moved = sum(v.size * v.dtype.itemsize for v in operands)
    moved += sum(int(np.prod(s.shape)) * s.dtype.itemsize for s in outs)
    return pl.pallas_call(
        kernel,
        name=name,
        out_shape=outs,
        in_specs=specs or [VMEM] * len(operands),
        out_specs=out_specs or [VMEM] * len(outs),
        scratch_shapes=scratch,
        compiler_params=pltpu.CompilerParams(vmem_limit_bytes=VMEM_MIB.get(name, 60) * 2**20),
        cost_estimate=pl.CostEstimate(flops=int(flops), bytes_accessed=moved, transcendentals=0),
    )(*operands)


def shaped(shape, dtype):
    return jax.ShapeDtypeStruct(shape, dtype)


def body(
    layer_input, out_grad, attention_norm_scale, expert_norm_scale, query_weight, key_weight,
    value_weight, output_weight, bias_table, router_weight, expert_in, expert_out, expert_ids,
    slot_ids, piece_ids, bucket_table,
):
    rows, width = layer_input.shape
    size = lax.axis_size("dp")
    seq = rows * 4
    heads = query_weight.shape[1] // HEAD_DIM
    experts = expert_in.shape[0]
    hidden = expert_in.shape[2]
    capacity = 2 * seq // experts
    head_count, bucket_count = bias_table.shape
    ring = use_ring(size)
    local = heads * HEAD_DIM
    span = query_weight.shape[0]
    count = size if ring else 1
    held = width // count
    groups = GROUPS

    (qkvo,) = call(
        "pack",
        pack_kernel,
        [shaped((span, 4 * local), BF)],
        [query_weight, key_weight, value_weight, output_weight],
    )
    packed = call(
        "pack_experts",
        functools.partial(pack_experts_kernel, groups),
        [shaped((2 * len(chosen), span, hidden), BF) for chosen in groups],
        [expert_in, jnp.transpose(expert_out, (0, 2, 1))],
    )
    buckets = jnp.pad(bucket_table, (0, 1), constant_values=-1).reshape(1, 2 * seq)
    info_rows, info_cols, wheel = call(
        "prepare",
        functools.partial(prepare_kernel, heads, experts, capacity),
        [shaped((8, seq), F32), shaped((seq, 8), F32), shaped((8, 2 * seq), F32)],
        [expert_ids.reshape(1, seq), piece_ids.reshape(1, seq), buckets, bias_table],
    )
    x_pieces = tensor_gather(layer_input, "gather_input", late=False)
    if ring:
        qkvo_chunks = ring_gather(
            qkvo, size, size // 2, "gather_qkvo", ((), tuple(packed), (info_rows, info_cols, wheel))
        )
        packed = [tie(v, qkvo_chunks[2], qkvo_chunks[6]) for v in packed]
        group_chunks = [
            ring_gather(v, size, size // 2 - 1 + g % 2, f"gather_experts{g}")
            for g, v in enumerate(packed)
        ]
    else:
        qkvo_chunks = [lax.all_gather(qkvo, "dp", axis=0, tiled=True)]
        group_chunks = [[lax.all_gather(v, "dp", axis=1, tiled=True)] for v in packed]
    g_pieces = tensor_gather(out_grad, "gather_cotangent")
    attn_gain = attention_norm_scale[None, :]
    moe_gain = expert_norm_scale[None, :]
    router = jnp.pad(router_weight, ((0, 0), (0, 128 - experts)))

    keep, send, qkv, ctx, lse, weight = call(
        "attention_forward", functools.partial(attention_forward_kernel, count, heads),
        [
            shaped((2, rows, width), BF), shaped((2, rows, width), BF), shaped((seq, 768), BF),
            shaped((seq, 256), BF), shaped((8, seq), F32), shaped((width, 1024), BF),
        ],
        [*x_pieces, attn_gain, wheel, info_rows, info_cols, *qkvo_chunks],
        [
            pltpu.VMEM((rows, 2 * seq), F32),
            pltpu.VMEM((4, rows, width), BF),
            pltpu.VMEM((seq, 128), F32),
        ],
        12e9,
    )
    if ring:
        send = tie(send, *(c[k] for c in group_chunks for k in (1, 7)), g_pieces[2])
    wait = (group_chunks[1][1], group_chunks[1][7]) if ring else ()
    a_parts = tensor_scatter(keep, send, "sum_attention")
    a_parts = (*a_parts[:2], tie(a_parts[2], *wait))
    resid_low = (
        layer_input.astype(F32)
        + (a_parts[0][0].astype(F32) + a_parts[1][0].astype(F32) + a_parts[2][0].astype(F32))
    ).astype(BF)
    if ring:
        resid_low = tie(resid_low, group_chunks[0][2], group_chunks[0][6])
    r_pieces = tensor_gather(resid_low, "gather_residual")

    expert_grads, group_grads, rings = [], [], []
    for g, chosen in enumerate(groups):
        first, last = g == 0, g == len(groups) - 1
        operands = [*r_pieces, moe_gain, info_rows, info_cols]
        if first:
            operands += [*g_pieces, router]
        else:
            operands += [normed_two, d_token, out_part, grad_part]
        results = moe_call(
            operands, group_chunks[g], chosen, first, last, (rows, width, hidden), experts, capacity
        )
        if first:
            normed_two, d_token, results = results[0], results[1], results[2:]
        if last:
            keep, send, moe_gain_grad, results = *results[:3], results[3:]
        else:
            out_part, grad_part, results = results[0], results[1], results[2:]
        if ring:
            hops = ring_scatter(results, size, size // 2 - 1 + g % 2, f"sum_grads{g}")
            next(hops)
            rings.append(hops)
            if first:
                early = hops.send(())
        else:
            total = lax.psum_scatter(results[0].astype(F32), "dp", scatter_dimension=1, tiled=True)
            expert_grads.append(total)
        group_grads.append(results)
    if ring:
        send = tie(send, *early)
    m_parts = tensor_scatter(keep, send, "sum_experts_d_resid")
    if ring:
        wait = (m_parts[1],)
        arrived = [hops.send(wait) for hops in rings]

    layer_output, d_resid, d_resid_low, small = call(
        "join", functools.partial(join_kernel, experts),
        [
            shaped((rows, width), BF), shaped((rows, width), F32), shaped((rows, width), BF),
            shaped((16, width), F32),
        ],
        [
            layer_input, *a_parts, *m_parts,
            out_grad, moe_gain, router, info_cols,
        ],
        flops=1e9,
    )
    if ring:
        arrived[0] = rings[0].send(())
    d_pieces = tensor_gather(d_resid_low, "gather_d_resid")
    if ring:
        wheel = tie(wheel, *arrived[1])
        arrived[1] = rings[1].send(())

    tiles = 7
    shared = [
        pltpu.VMEM((seq, 128), BF),
        pltpu.VMEM((seq, 128), F32),
        pltpu.VMEM((seq, 128), F32),
        pltpu.VMEM((seq, 128), F32),
        pltpu.VMEM((rows, 2 * seq), F32),
        pltpu.VMEM((tiles, rows, rows), F32),
        pltpu.VMEM((tiles, rows, rows), F32),
    ]
    operands = [*d_pieces, wheel, buckets, info_rows, info_cols, qkv, ctx, lse, weight]
    d_part, bias_grad = call(
        "attention_backward0",
        functools.partial(attention_backward_kernel, count, heads, 0),
        [shaped((seq, 384), BF), shaped((bucket_count, 128), F32)],
        operands,
        shared,
        12e9,
    )
    if ring:
        wait = (d_part,)
        d_part = tie(d_part, *arrived[0])
        arrived[0] = rings[0].send(wait)
    d_qkv, bias_grad, *qkvo_grads = call(
        "attention_backward1",
        functools.partial(attention_backward_kernel, count, heads, 1),
        [
            shaped((seq, 768), BF), shaped((bucket_count, 128), F32),
            *[shaped((held + SMALL * ring, 4 * local), BF)] * count,
        ],
        [*operands, *x_pieces, attn_gain, d_part, bias_grad],
        [
            pltpu.VMEM((width, 4 * local), F32),
            pltpu.VMEM((seq, width), BF),
            pltpu.VMEM((seq, width), BF),
            *shared,
        ],
        12e9,
    )
    if ring:
        wait = (d_qkv,)
        d_qkv = tie(d_qkv, *arrived[1], *arrived[0])
        arrived[1] = rings[1].send(wait)
    keep, send, sums = call(
        "input_share", functools.partial(input_share_kernel, experts),
        [
            shaped((2, rows, width), BF), shaped((2, rows, width), BF), shaped((SMALL, width), F32),
        ],
        [*x_pieces, attn_gain, d_qkv, weight, small, moe_gain_grad, bias_grad],
        flops=2e9,
    )
    if ring:
        arrived[1] = rings[1].send(())
    i0, i1, i2 = tensor_scatter(keep, send, "sum_input_grad")
    input_grad = (
        d_resid + (i0[0].astype(F32) + i1[0].astype(F32) + i2[0].astype(F32))
    ).astype(BF)
    if ring:
        own = jnp.pad(sums.astype(BF), ((held, 0), (0, 0)))
        sent = [v + own if k in (3, 4) else v for k, v in enumerate(qkvo_grads)]
        hops = ring_scatter(sent, size, 3, "sum_grads_qkvo")
        next(hops)
        sums = own[held:].astype(F32)
        for hop in range(4):
            qkvo_up, qkvo_down = hops.send((i1,) if hop == 1 else ())
            if hop == 2:
                qkvo_late = qkvo_down
            sums = sums + qkvo_down[held:].astype(F32)
            if hop < 3:
                sums = sums + qkvo_up[held:].astype(F32)
    else:
        sums = lax.psum(sums, "dp")
    sums = sums + swap(sums, 1)
    sums = sums + swap(sums, 2)
    grad_attn_gain, grad_moe_gain = sums[0], sums[1]
    grad_router = jnp.transpose(sums[2 : 2 + experts])
    grad_bias_table = jnp.transpose(
        jnp.concatenate(
            [sums[8:16, i * 128 : i * 128 + head_count] for i in range(bucket_count // 8)], axis=0
        )
    )
    if ring:
        qkvo_grad = (
            qkvo_grads[0].astype(F32) + qkvo_up.astype(F32) + qkvo_down.astype(F32)
        )[:held]
        group_grads[0] = [tie(group_grads[0][0], qkvo_late)]
        grad_in, grad_out = call(
            "finish",
            functools.partial(finish_kernel, groups),
            [shaped((experts, span, hidden), F32)] * 2,
            [v for parts, came in zip(group_grads, arrived) for v in (parts[0], *came)],
        )
    else:
        qkvo_grad = lax.psum_scatter(
            qkvo_grads[0].astype(F32), "dp", scatter_dimension=0, tiled=True
        )
        kinds = [len(chosen) for chosen in groups]
        grad_in = jnp.concatenate([v[:n] for v, n in zip(expert_grads, kinds)], axis=0)
        grad_out = jnp.concatenate([v[n:] for v, n in zip(expert_grads, kinds)], axis=0)
    grad_query, grad_key, grad_value = (
        qkvo_grad[:, s * local : (s + 1) * local] for s in range(3)
    )
    grad_output = jnp.transpose(qkvo_grad[:, 3 * local :])
    grad_out = jnp.transpose(grad_out, (0, 2, 1))
    return (
        layer_output, input_grad, grad_attn_gain, grad_moe_gain, grad_query, grad_key, grad_value,
        grad_output, grad_bias_table, grad_router, grad_in, grad_out,
    )


def solution(mesh):
    in_specs = (
        P(("dp", "tensor"), None),
        P(("dp", "tensor"), None),
        P(),
        P(),
        P("dp", "tensor"),
        P("dp", "tensor"),
        P("dp", "tensor"),
        P("tensor", "dp"),
        P(),
        P(),
        P(None, "dp", "tensor"),
        P(None, "tensor", "dp"),
        P("dp"),
        P("dp"),
        P("dp"),
        P(),
    )
    out_specs = (
        P(("dp", "tensor"), None),
        P(("dp", "tensor"), None),
        P(),
        P(),
        P("dp", "tensor"),
        P("dp", "tensor"),
        P("dp", "tensor"),
        P("tensor", "dp"),
        P(),
        P(),
        P(None, "dp", "tensor"),
        P(None, "tensor", "dp"),
    )
    return jax.shard_map(body, mesh=mesh, in_specs=in_specs, out_specs=out_specs, check_vma=False)
```
